32 devices in a mesh: parts: 2 (over y), dp: 4 (over z), tensor: 4 (over x, core).
Axes of the slice: x: 2, y: 2, z: 4, core: 2. Of those that a mesh axis runs over, the one named last changes fastest.
Arguments:
- hidden_in: bfloat16 [4096, 4096], P(('parts', 'dp'), 'tensor'), parts along dimension 0, may hold values from -80 to 80
- row_loads: int32 [8, 4], P(('parts', 'dp')), parts along dimension 0, may hold values from 0 to 256, as said below
- seg_ids: int32 [4096], P(('parts', 'dp')), parts along dimension 0, may hold values from 0 to 3, as said below
- pos_ids: int32 [4096], P(('parts', 'dp')), parts along dimension 0, may hold values from 0 to 511, as said below
- prompt_order: int32 [8, 512], P(('parts', 'dp')), parts along dimension 0, may hold values from 0 to 511, each once within a row
- attn_gain: bfloat16 [4096], replicated, may hold values from 0.099609375 to 1.8984375
- w_query: bfloat16 [4096, 2048], P(None, 'tensor'), may hold values from -2 to 2
- key_matrix: bfloat16 [4096, 512], P(None, 'tensor'), may hold values from -2 to 2
- value_matrix: bfloat16 [4096, 512], P(None, 'tensor'), may hold values from -0.09375 to 0.09375
- w_out: bfloat16 [2048, 4096], P('tensor'), may hold values from -0.125 to 0.125
- final_gain: bfloat16 [4096], P('tensor'), may hold values from 0.099609375 to 1.8984375
- value_head: bfloat16 [4096], P('tensor'), may hold values from -0.09375 to 0.09375
Outputs:
- hidden_out: bfloat16 [4096, 4096], P(('parts', 'dp'), 'tensor'), parts along dimension 0
- token_values: float32 [4096], P(('parts', 'dp')), parts along dimension 0
The draws below stay inside these ranges and needn't reach their ends.
There are 2 independent parts, one for each index of `parts`. The reference program is written for one: setup_inputs(seed, part) draws one part's arguments, and reference() takes and returns one part's arrays. A program takes and returns all parts, laid end to end along the dimension named above; an argument that names none is the same for every part. Nothing has to cross between parts.
Inputs may be any that keep to these rules, and one draw needn't show every extreme that they name: `row_loads`: row s lists how many rows of shard s go to each destination shard, in destination order; each row sums to 512, and one destination receives exactly 256 rows from every shard. `seg_ids`: over one destination's rows, taken in shard order and then in row order, ids never fall; rows with one id there form one document. `pos_ids`: A row's position counts the earlier rows of its document in that order.
All inputs are finite; a program needn't handle non-finite values.
Results may differ from the reference program's by a relative error of at most 0.005.
Values may be sent and summed in bfloat16 or wider, within the bound.
No kernel may reach another device: no remote copies, remote signals or barrier semaphores. Data moves between devices by JAX's collectives and lax.ppermute only.
A program may use at most 128 MiB of HBM per device.

```python
import math
import jax
import jax.numpy as jnp
from jax import lax

MODEL_WIDTH = 4096
QUERY_HEADS = 16
KEY_VALUE_HEADS = 4
HEAD_WIDTH = 128
TOK_DEV = 512
SLOT = 256
TOKENS = 2048
N_DP = 4


def shuffle_one(one_key):
    return jax.random.permutation(one_key, N_DP - 1)


def doc_starts(one_key):
    stream_len = N_DP * SLOT
    long_len = stream_len // 2
    picked = jax.random.permutation(one_key, stream_len - long_len - 1)[:N_DP - 2] + long_len + 1
    return jnp.zeros((stream_len,), jnp.int32).at[picked].set(1).at[long_len].set(1)


def stream_layout(key):
    key_dest, key_perm, key_shift, key_flags = jax.random.split(key, 4)
    half_load = SLOT // 2
    dest_full = jax.random.randint(key_dest, (), 0, N_DP)
    perm_keys = jax.random.split(key_perm, N_DP)
    others = jax.vmap(shuffle_one)(perm_keys).astype(jnp.int32) + 1
    offsets = jnp.concatenate([jnp.zeros((N_DP, 1), jnp.int32), others], 1)
    columns = (dest_full + offsets) % N_DP
    shifts = jax.random.randint(key_shift, (N_DP, N_DP // 2), 0, half_load + 1)
    shifts = shifts.at[:, 0].set(half_load)
    amounts = jnp.stack([half_load + shifts, half_load - shifts], 2).reshape(N_DP, N_DP).astype(jnp.int32)
    sources = jnp.broadcast_to(jnp.arange(N_DP)[:, None], (N_DP, N_DP))
    row_loads = jnp.zeros((N_DP, N_DP), jnp.int32).at[sources, columns].set(amounts)
    stream_len = N_DP * SLOT
    flags = jax.vmap(doc_starts)(jax.random.split(key_flags, N_DP)).astype(jnp.int32)
    seg_stream = jnp.cumsum(flags, 1).astype(jnp.int32)
    lane_ids = jnp.arange(SLOT)
    used = (lane_ids[None, None, :] < row_loads.T[:, :, None]).astype(jnp.int32).reshape(N_DP, stream_len)
    before = (jnp.cumsum(used, 1) - used).astype(jnp.int32)
    starting = jnp.concatenate([jnp.ones((N_DP, 1), bool), seg_stream[:, 1:] != seg_stream[:, :-1]], 1)
    base_count = lax.cummax(jnp.where(starting, before, 0), axis=1)
    pos_stream = (before - base_count).astype(jnp.int32)
    block_end = jnp.cumsum(row_loads, 1).astype(jnp.int32)
    block_start = block_end - row_loads
    row_ids = jnp.arange(TOK_DEV)
    dest_of = jnp.sum((block_end[:, None, :] <= row_ids[None, :, None]).astype(jnp.int32), 2).astype(jnp.int32)
    lane_of = row_ids[None, :] - jnp.take_along_axis(block_start, dest_of, 1)
    slot_of = jnp.arange(N_DP)[:, None] * SLOT + lane_of
    seg_source = seg_stream[dest_of, slot_of]
    pos_source = pos_stream[dest_of, slot_of]
    return (row_loads, seg_source.reshape(TOKENS).astype(jnp.int32), pos_source.reshape(TOKENS).astype(jnp.int32))


def draw_row_loads(key, part):
    return stream_layout(key)[0]


def draw_seg_ids(key, part):
    return stream_layout(key)[1]


def draw_pos_ids(key, part):
    return stream_layout(key)[2]


def draw_hidden_in(key, part):
    key = jax.random.fold_in(key, 7)
    key_main, key_rows, key_cols = jax.random.split(key, 3)
    column_index = jnp.arange(MODEL_WIDTH, dtype=jnp.float32) / MODEL_WIDTH
    main = jnp.clip(jax.random.normal(key_main, (TOKENS, MODEL_WIDTH), jnp.float32), -5.0, 5.0)
    row_scale = jnp.exp(jax.random.uniform(key_rows, (TOKENS, 1), jnp.float32, 0.0, math.log(10.0)))
    column_scale = 10.0 ** (column_index - 1.0)
    jitter = jnp.exp(jax.random.uniform(key_cols, (1, MODEL_WIDTH), jnp.float32, -0.35, 0.35))
    return (main * row_scale * column_scale[None, :] * jitter).astype(jnp.bfloat16)


def draw_key_matrix(key, part):
    key = jax.random.fold_in(key, 21)
    reward_output = jnp.clip(jax.random.normal(key, (MODEL_WIDTH, KEY_VALUE_HEADS * HEAD_WIDTH), jnp.float32), -6.0, 6.0) / math.sqrt(MODEL_WIDTH)
    return reward_output.astype(jnp.bfloat16)


def draw_w_query(key, part):
    key = jax.random.fold_in(key, 22)
    local_rows = jnp.clip(jax.random.normal(key, (MODEL_WIDTH, QUERY_HEADS * HEAD_WIDTH), jnp.float32), -6.0, 6.0)
    return (local_rows / math.sqrt(MODEL_WIDTH)).astype(jnp.bfloat16)


def steps_of(own_key, shape, shards, low, high):
    def one(position, shards_of):
        heights = jax.random.uniform(jax.random.fold_in(jax.random.fold_in(own_key, 6), position), (shards_of,), jnp.float32, low / len(shards), high / len(shards))
        return jnp.repeat(jnp.exp(heights), shape[position] // shards_of).reshape((-1,) + (1,) * (len(shape) - position - 1))

    loudness = one(*shards[0])
    for cut in shards[1:]:
        loudness = loudness * one(*cut)
    return loudness


def centred(rng, shape, scale, reach, cuts=(), held_as=jnp.bfloat16):
    entries = jax.random.normal(rng, shape, jnp.float32) * scale
    if len(cuts) > 0:
        entries = steps_of(rng, shape, cuts, -0.22, 0.18) * entries
    return jnp.clip(entries, min=-reach, max=reach).astype(held_as)


def setup_inputs(seed: int = 0, part: int = 0) -> dict:
    arg_keys = jax.random.split(jax.random.key(seed), 13)
    part_keys = jax.random.split(jax.random.fold_in(arg_keys[12], part), 13)
    hidden_in = draw_hidden_in(jax.random.fold_in(jax.random.fold_in(arg_keys[12], part), 71), part)
    row_loads = draw_row_loads(jax.random.fold_in(jax.random.fold_in(arg_keys[12], part), 71), part)
    seg_ids = draw_seg_ids(jax.random.fold_in(jax.random.fold_in(arg_keys[12], part), 71), part)
    pos_ids = draw_pos_ids(jax.random.fold_in(jax.random.fold_in(arg_keys[12], part), 71), part)
    prompt_order = jax.vmap(lambda own: jax.random.permutation(own, TOK_DEV))(jax.random.split(part_keys[4], N_DP)).reshape((N_DP, TOK_DEV)).astype(jnp.int32)
    attn_gain = jnp.clip(1.0 + 0.18 * jax.random.normal(arg_keys[5], (MODEL_WIDTH,), jnp.float32), 0.099609375, 1.8984375).astype(jnp.bfloat16)
    w_query = draw_w_query(jax.random.fold_in(arg_keys[12], 71), part)
    key_matrix = draw_key_matrix(jax.random.fold_in(arg_keys[12], 71), part)
    value_matrix = centred(arg_keys[8], (MODEL_WIDTH, KEY_VALUE_HEADS * HEAD_WIDTH), MODEL_WIDTH ** -0.5, 0.09375, ((1, 4),))
    w_out = centred(arg_keys[9], (QUERY_HEADS * HEAD_WIDTH, MODEL_WIDTH), (QUERY_HEADS * HEAD_WIDTH) ** -0.5, 0.125, ((0, 4),))
    final_gain = jnp.clip(1.0 + 0.18 * jax.random.normal(arg_keys[10], (MODEL_WIDTH,), jnp.float32), 0.099609375, 1.8984375).astype(jnp.bfloat16)
    value_head = centred(arg_keys[11], (MODEL_WIDTH,), MODEL_WIDTH ** -0.5, 0.09375, ((0, 4),))
    return {"hidden_in": hidden_in, "row_loads": row_loads, "seg_ids": seg_ids, "pos_ids": pos_ids, "prompt_order": prompt_order, "attn_gain": attn_gain, "w_query": w_query, "key_matrix": key_matrix, "value_matrix": value_matrix, "w_out": w_out, "final_gain": final_gain, "value_head": value_head}


norm_eps = 1e-05
rope_base = 500000.0

def rotary_embed(vectors, positions):
    head_size = vectors.shape[-1]
    half_size = head_size // 2
    inverse = rope_base ** (-(jnp.arange(half_size, dtype=jnp.float32) * 2.0) / head_size)
    angles = positions.astype(jnp.float32)[..., None] * inverse
    cosine = jnp.cos(angles)[..., None, :]
    sine_part = jnp.sin(angles)[..., None, :]
    first_half = vectors[..., :half_size]
    second_half = vectors[..., half_size:]
    return jnp.concatenate([first_half * cosine - second_half * sine_part, second_half * cosine + first_half * sine_part], -1)

def score_stream(rows, seg_slots, position_slots, params):
    attn_gain, w_query, key_matrix, value_matrix, w_out, final_gain, value_head = params
    total_slots = rows.shape[0]
    as_float = rows.astype(jnp.float32)
    normed_hidden = (as_float * lax.rsqrt(lax.optimization_barrier(jnp.mean(as_float * as_float, -1, keepdims=True)) + norm_eps) * attn_gain.astype(jnp.float32)).astype(jnp.bfloat16)
    query_rows = rotary_embed(jnp.dot(normed_hidden, w_query, preferred_element_type=jnp.float32).reshape(total_slots, QUERY_HEADS, HEAD_WIDTH), position_slots).astype(jnp.bfloat16)
    key_head_rows = rotary_embed(jnp.dot(normed_hidden, key_matrix, preferred_element_type=jnp.float32).reshape(total_slots, KEY_VALUE_HEADS, HEAD_WIDTH), position_slots).astype(jnp.bfloat16)
    value_head_rows = jnp.dot(normed_hidden, value_matrix, preferred_element_type=jnp.float32).astype(jnp.bfloat16).reshape(total_slots, KEY_VALUE_HEADS, HEAD_WIDTH)
    heads_per_group = QUERY_HEADS // KEY_VALUE_HEADS
    query_group_rows = query_rows.astype(jnp.float32).reshape(total_slots, KEY_VALUE_HEADS, heads_per_group, HEAD_WIDTH)
    scores = jnp.einsum('qgjd,kgd->gjqk', query_group_rows, key_head_rows.astype(jnp.float32)) / HEAD_WIDTH ** 0.5
    slot_ids = jnp.arange(total_slots)
    allowed = (seg_slots[:, None] == seg_slots[None, :]) & (slot_ids[None, :] <= slot_ids[:, None])
    scores = jnp.where(allowed, scores, -jnp.inf)
    row_max = lax.optimization_barrier(jnp.max(scores, -1, keepdims=True))
    exp_terms = jnp.where(allowed, jnp.exp(scores - row_max), 0.0)
    probabilities = (exp_terms / lax.optimization_barrier(jnp.sum(exp_terms, -1, keepdims=True))).astype(jnp.bfloat16)
    mixed_heads = jnp.einsum('gjqk,kgd->qgjd', probabilities.astype(jnp.float32), value_head_rows.astype(jnp.float32)).astype(jnp.bfloat16).reshape(total_slots, QUERY_HEADS * HEAD_WIDTH)
    attended = jnp.dot(mixed_heads, w_out, preferred_element_type=jnp.float32)
    hidden = (as_float + attended).astype(jnp.bfloat16)
    hidden_float = hidden.astype(jnp.float32)
    square_sum = lax.optimization_barrier(jnp.sum(hidden_float * hidden_float, -1))
    head_dot = lax.optimization_barrier(jnp.sum(hidden_float * final_gain.astype(jnp.float32) * value_head.astype(jnp.float32), -1))
    return (hidden, head_dot * lax.rsqrt(square_sum / MODEL_WIDTH + norm_eps))

def reference(hidden_in, row_loads, seg_ids, pos_ids, prompt_order, attn_gain, w_query, key_matrix, value_matrix, w_out, final_gain, value_head):
    rows_all = hidden_in.reshape(N_DP, TOK_DEV, MODEL_WIDTH)
    segs_all = seg_ids.reshape(N_DP, TOK_DEV)
    poss_all = pos_ids.reshape(N_DP, TOK_DEV)
    block_end = jnp.cumsum(row_loads, 1).astype(jnp.int32)
    block_start = (block_end - row_loads).astype(jnp.int32)
    lane_ids = jnp.arange(SLOT, dtype=jnp.int32)
    sources = jnp.arange(N_DP, dtype=jnp.int32)
    params = (attn_gain, w_query, key_matrix, value_matrix, w_out, final_gain, value_head)

    def one_dest(dest):
        amount = row_loads[:, dest]
        is_used = lane_ids[None, :] < amount[:, None]
        row_index = jnp.minimum(block_start[:, dest][:, None] + lane_ids[None, :], TOK_DEV - 1).astype(jnp.int32)
        rows = jnp.where(is_used[:, :, None], rows_all[sources[:, None], row_index], 0)
        seg_slots = jnp.where(is_used, segs_all[sources[:, None], row_index], -1)
        position_slots = jnp.where(is_used, poss_all[sources[:, None], row_index], 0)
        hidden, values = score_stream(rows.reshape(N_DP * SLOT, MODEL_WIDTH), seg_slots.reshape(N_DP * SLOT), position_slots.reshape(N_DP * SLOT), params)
        return (hidden.reshape(N_DP, SLOT, MODEL_WIDTH), values.reshape(N_DP, SLOT))
    hidden_all, values_all = lax.map(one_dest, jnp.arange(N_DP, dtype=jnp.int32))
    row_ids = jnp.arange(TOK_DEV, dtype=jnp.int32)
    dest_of = lax.optimization_barrier(jnp.sum((block_end[:, None, :] <= row_ids[None, :, None]).astype(jnp.int32), 2)).astype(jnp.int32)
    lane_of = (row_ids[None, :] - jnp.take_along_axis(block_start, dest_of, 1)).astype(jnp.int32)
    pick_dest = jnp.take_along_axis(dest_of, prompt_order, 1)
    pick_lane = jnp.take_along_axis(lane_of, prompt_order, 1)
    hidden_out = hidden_all[pick_dest, sources[:, None], pick_lane].reshape(TOKENS, MODEL_WIDTH)
    token_values = values_all[pick_dest, sources[:, None], pick_lane].reshape(TOKENS)
    return (hidden_out, token_values)
```

```python
import functools

import jax
import jax.numpy as jnp
from jax import lax
from jax.experimental import pallas as pl
from jax.experimental.pallas import tpu as pltpu
from jax.sharding import PartitionSpec as P

MODEL_WIDTH = 4096
HEAD_WIDTH = 128
NORM_EPS = 1e-05
ROPE_BASE = 500000.0

SEG_SPAN = 64
POS_SPAN = 1024

QUERY_BLOCK = 128
KEY_BLOCK = 256
MASKED = -1e30

VMEM = pltpu.VMEM


def params(limit_mib):
    return pltpu.CompilerParams(vmem_limit_bytes=limit_mib * 2**20)


def whole():
    return pl.BlockSpec(memory_space=VMEM)


def qkv_kernel(ids, r0, r1, r2, r3, gain, wq, wk, wv, cos, sin, q_out, kv_out):
    pieces = (r0, r1, r2, r3)
    width = r0.shape[1]
    square = jnp.zeros((r0.shape[0], 1), jnp.float32)
    for piece in pieces:
        x = piece[...].astype(jnp.float32)
        square += jnp.sum(x * x, -1, keepdims=True)
    scale = lax.rsqrt(square / MODEL_WIDTH + NORM_EPS)
    q = k = v = None
    for i, piece in enumerate(pieces):
        own = ids[i]
        x = piece[...].astype(jnp.float32)
        normed = (x * scale * gain[pl.ds(own, 1), :]).astype(jnp.bfloat16)
        at = pl.ds(pl.multiple_of(own * width, width), width)
        qi = jnp.dot(normed, wq[at, :], preferred_element_type=jnp.float32)
        ki = jnp.dot(normed, wk[at, :], preferred_element_type=jnp.float32)
        vi = jnp.dot(normed, wv[at, :], preferred_element_type=jnp.float32)
        q, k, v = (qi, ki, vi) if i == 0 else (q + qi, k + ki, v + vi)

    def rope(x):
        return (x * cos[...] + pltpu.roll(x, HEAD_WIDTH // 2, 1) * sin[...]).astype(jnp.bfloat16)

    for h in range(q_out.shape[0]):
        q_out[h] = rope(q[:, h * HEAD_WIDTH : (h + 1) * HEAD_WIDTH])
    kv_out[:, :HEAD_WIDTH] = rope(k)
    kv_out[:, HEAD_WIDTH:] = v.astype(jnp.bfloat16)


def qkv(ids, pieces, gain, wq, wk, wv, cos, sin):
    rows = pieces[0].shape[0]
    heads = wq.shape[1] // HEAD_WIDTH
    return pl.pallas_call(
        qkv_kernel,
        out_shape=(
            jax.ShapeDtypeStruct((heads, rows, HEAD_WIDTH), jnp.bfloat16),
            jax.ShapeDtypeStruct((rows, 2 * HEAD_WIDTH), jnp.bfloat16),
        ),
        in_specs=[pl.BlockSpec(memory_space=pltpu.SMEM)] + [whole()] * 10,
        out_specs=(whole(), whole()),
        compiler_params=params(24),
        cost_estimate=pl.CostEstimate(
            flops=2 * rows * MODEL_WIDTH * (wq.shape[1] + 2 * HEAD_WIDTH),
            bytes_accessed=MODEL_WIDTH * 2 * (rows + wq.shape[1] + 2 * HEAD_WIDTH),
            transcendentals=0,
        ),
        name="qkv",
    )(ids, *pieces, gain, wq, wk, wv, cos, sin)


def attend_kernel(n_chunk, n_shard, begin, end, *refs):
    q_in = refs[:n_chunk]
    kv_in = refs[n_chunk : n_chunk + n_chunk * n_shard]
    key_q, low_q, key_k, order, out, q_all, kv_all, heads, m_s, l_s, acc_s, sem = refs[
        n_chunk + n_chunk * n_shard :
    ]
    n_head, rows, _ = q_all.shape
    step = rows // n_chunk
    copies = []
    for c in range(n_chunk):
        copies.append(pltpu.make_async_copy(q_in[c], q_all.at[:, pl.ds(c * step, step), :], sem.at[c]))
    for i in range(n_chunk * n_shard):
        copies.append(
            pltpu.make_async_copy(kv_in[i], kv_all.at[pl.ds(i * step, step), :], sem.at[n_chunk + i])
        )
    for copy in copies:
        copy.start()
    for copy in copies:
        copy.wait()
    scale = 1.4426950408889634 / HEAD_WIDTH**0.5
    stacked = n_head * QUERY_BLOCK
    per_shard = rows // KEY_BLOCK

    def block(qb, _):
        at = pl.ds(pl.multiple_of(qb * QUERY_BLOCK, QUERY_BLOCK), QUERY_BLOCK)
        q = q_all[:, at, :].reshape(stacked, HEAD_WIDTH)
        high = key_q[at, :]
        low = low_q[at, :]
        m_s[...] = jnp.full(m_s.shape, MASKED, jnp.float32)
        l_s[...] = jnp.zeros(l_s.shape, jnp.float32)
        acc_s[...] = jnp.zeros(acc_s.shape, jnp.float32)

        def shard(d, _):
            def keys(kb, _):
                index = d * per_shard + kb
                span = pl.ds(pl.multiple_of(index * KEY_BLOCK, KEY_BLOCK), KEY_BLOCK)
                k = kv_all[span, :HEAD_WIDTH]
                v = kv_all[span, HEAD_WIDTH:]
                s = lax.dot_general(q, k, (((1,), (1,)), ((), ())), preferred_element_type=jnp.float32)
                ids = key_k[pl.ds(index, 1), :]
                allowed = (ids <= high) & (ids >= low)
                s = jnp.where(allowed[None], (s * scale).reshape(n_head, QUERY_BLOCK, KEY_BLOCK), MASKED)
                s = s.reshape(stacked, KEY_BLOCK)
                m_old = m_s[...]
                m_new = jnp.maximum(m_old, jnp.max(s, -1, keepdims=True))
                alpha = jnp.exp2(m_old - m_new)
                p = [
                    jnp.exp2(s[:, i : i + HEAD_WIDTH] - m_new) for i in range(0, KEY_BLOCK, HEAD_WIDTH)
                ]
                m_s[...] = m_new
                l_s[...] = l_s[...] * alpha + functools.reduce(jnp.add, p)
                p = jnp.concatenate(p, 1).astype(jnp.bfloat16)
                acc_s[...] = acc_s[...] * alpha + jnp.dot(p, v, preferred_element_type=jnp.float32)
                return 0

            return lax.fori_loop(begin[qb, d], end[qb, d], keys, 0)

        lax.fori_loop(0, n_shard, shard, 0)
        done = (acc_s[...] / jnp.sum(l_s[...], -1, keepdims=True)).astype(jnp.bfloat16)
        for h in range(n_head):
            heads[at, h * HEAD_WIDTH : (h + 1) * HEAD_WIDTH] = done[h * QUERY_BLOCK : (h + 1) * QUERY_BLOCK]
        return 0

    lax.fori_loop(0, rows // QUERY_BLOCK, block, 0)
    pick = (order[...] == lax.broadcasted_iota(jnp.int32, (rows, rows), 1)).astype(jnp.bfloat16)
    out[...] = jnp.dot(pick, heads[...], preferred_element_type=jnp.float32).astype(jnp.bfloat16)


def attend(begin, end, q_parts, kv_parts, key_q, low_q, key_k, order):
    n_chunk = len(q_parts)
    n_shard = len(kv_parts) // n_chunk
    n_head, step, _ = q_parts[0].shape
    rows = step * n_chunk
    stacked = n_head * QUERY_BLOCK
    smem = pl.BlockSpec(memory_space=pltpu.SMEM)
    return pl.pallas_call(
        functools.partial(attend_kernel, n_chunk, n_shard),
        out_shape=jax.ShapeDtypeStruct((rows, n_head * HEAD_WIDTH), jnp.bfloat16),
        in_specs=[smem, smem]
        + [pl.BlockSpec(memory_space=pl.ANY)] * (len(q_parts) + len(kv_parts))
        + [whole()] * 4,
        out_specs=whole(),
        scratch_shapes=[
            VMEM((n_head, rows, HEAD_WIDTH), jnp.bfloat16),
            VMEM((n_shard * rows, 2 * HEAD_WIDTH), jnp.bfloat16),
            VMEM((rows, n_head * HEAD_WIDTH), jnp.bfloat16),
            VMEM((stacked, HEAD_WIDTH), jnp.float32),
            VMEM((stacked, HEAD_WIDTH), jnp.float32),
            VMEM((stacked, HEAD_WIDTH), jnp.float32),
            pltpu.SemaphoreType.DMA((len(q_parts) + len(kv_parts),)),
        ],
        compiler_params=params(32),
        cost_estimate=pl.CostEstimate(
            flops=4 * rows * rows * n_shard * n_head * HEAD_WIDTH,
            bytes_accessed=4 * rows * n_head * HEAD_WIDTH + 4 * rows * n_shard * HEAD_WIDTH,
            transcendentals=rows * rows * n_shard * n_head,
        ),
        name="attend",
    )(begin, end, *q_parts, *kv_parts, key_q, low_q, key_k, order)


def project_kernel(ids, h0, h1, w0, w1, out):
    total = jnp.dot(h0[...], w0[...], preferred_element_type=jnp.float32)
    total += jnp.dot(h1[...], w1[...], preferred_element_type=jnp.float32)
    out[...] = total.astype(out.dtype)


def project(ids, h0, h1, w0, w1, width, part, n_part):
    rows, depth = h0.shape
    step = rows // n_part
    return pl.pallas_call(
        project_kernel,
        grid_spec=pltpu.PrefetchScalarGridSpec(
            num_scalar_prefetch=1,
            grid=(1,),
            in_specs=[
                pl.BlockSpec((step, depth), lambda i, ids: (part, 0)),
                pl.BlockSpec((step, depth), lambda i, ids: (part, 0)),
                pl.BlockSpec((depth, width), lambda i, ids: (0, ids[0])),
                pl.BlockSpec((depth, width), lambda i, ids: (0, ids[1])),
            ],
            out_specs=pl.BlockSpec((step, width), lambda i, ids: (0, 0)),
        ),
        out_shape=jax.ShapeDtypeStruct((step, width), jnp.bfloat16),
        compiler_params=params(24),
        cost_estimate=pl.CostEstimate(
            flops=4 * step * depth * width, bytes_accessed=4 * depth * width, transcendentals=0
        ),
        name="project",
    )(ids, h0, h1, w0, w1)


def keep_kernel(ids, order, own, h0, h1, w0, w1, out):
    rows = own.shape[0]
    pick = (order[...] == lax.broadcasted_iota(jnp.int32, (rows, rows), 1)).astype(jnp.bfloat16)
    total = jnp.dot(h0[...], w0[...], preferred_element_type=jnp.float32)
    total += jnp.dot(h1[...], w1[...], preferred_element_type=jnp.float32)
    out[...] = total + jnp.dot(pick, own[...], preferred_element_type=jnp.float32)


def keep(ids, order, own, h0, h1, w0, w1):
    rows, width = own.shape
    depth = h0.shape[1]
    return pl.pallas_call(
        keep_kernel,
        grid_spec=pltpu.PrefetchScalarGridSpec(
            num_scalar_prefetch=1,
            grid=(1,),
            in_specs=[
                pl.BlockSpec((rows, 1), lambda i, ids: (0, 0)),
                pl.BlockSpec((rows, width), lambda i, ids: (0, 0)),
                pl.BlockSpec((rows, depth), lambda i, ids: (0, 0)),
                pl.BlockSpec((rows, depth), lambda i, ids: (0, 0)),
                pl.BlockSpec((depth, width), lambda i, ids: (0, ids[0])),
                pl.BlockSpec((depth, width), lambda i, ids: (0, ids[1])),
            ],
            out_specs=pl.BlockSpec((rows, width), lambda i, ids: (0, 0)),
        ),
        out_shape=jax.ShapeDtypeStruct((rows, width), jnp.float32),
        compiler_params=params(32),
        cost_estimate=pl.CostEstimate(
            flops=2 * rows * (2 * depth + rows) * width,
            bytes_accessed=4 * depth * width + 6 * rows * width,
            transcendentals=0,
        ),
        name="keep",
    )(ids, order, own, h0, h1, w0, w1)


def finish_kernel(kept, received, gain, head, *refs):
    hidden_out, sums = refs[-2:]
    hidden = (kept[...] + received[...].astype(jnp.float32)).astype(jnp.bfloat16)
    hidden_out[...] = hidden
    x = hidden.astype(jnp.float32)
    weighted = x * (gain[...] * head[...])
    squared = x * x
    for i, terms in enumerate((squared, weighted)):
        lanes = functools.reduce(
            jnp.add, [terms[:, j : j + 128] for j in range(0, terms.shape[1], 128)]
        )
        sums[i : i + 1, :] = jnp.sum(lanes.T, 0, keepdims=True)


def finish(kept, received, gain, head, part, n_part, hidden):
    rows, width = kept.shape
    step = rows // n_part
    specs = [
        pl.BlockSpec((step, width), lambda i: (part, 0)),
        pl.BlockSpec((step, width), lambda i: (0, 0)),
        pl.BlockSpec((1, width), lambda i: (0, 0)),
        pl.BlockSpec((1, width), lambda i: (0, 0)),
    ]
    args = [kept, received, gain, head]
    aliases = {}
    if hidden is not None:
        specs.append(pl.BlockSpec(memory_space=pl.ANY))
        args.append(hidden)
        aliases = {4: 0}
    return pl.pallas_call(
        finish_kernel,
        grid=(1,),
        in_specs=specs,
        out_specs=(
            pl.BlockSpec((step, width), lambda i: (part, 0)),
            pl.BlockSpec((2, step), lambda i: (0, 0)),
        ),
        out_shape=(
            jax.ShapeDtypeStruct((rows, width), jnp.bfloat16),
            jax.ShapeDtypeStruct((2, step), jnp.float32),
        ),
        input_output_aliases=aliases,
        compiler_params=params(24),
        cost_estimate=pl.CostEstimate(
            flops=6 * step * width, bytes_accessed=8 * step * width, transcendentals=0
        ),
        name="finish",
    )(*args)


def flip(x, bit):
    count = lax.axis_size("tensor")
    return lax.ppermute(x, "tensor", [(i, i ^ bit) for i in range(count)])


def on_device(
    hidden_in,
    row_loads,
    seg_ids,
    pos_ids,
    prompt_order,
    attn_gain,
    w_query,
    key_matrix,
    value_matrix,
    w_out,
    final_gain,
    value_head,
):
    n_dp = lax.axis_size("dp")
    me = lax.axis_index("dp")
    t = lax.axis_index("tensor")
    rows, width = hidden_in.shape
    n_chunk = 4 if n_dp <= 8 else 1
    n_part = 2
    step = rows // n_chunk

    w_blocks = w_out.reshape(w_out.shape[0], 2, 2, width)
    w_send = lax.dynamic_index_in_dim(w_blocks, 1 - t % 2, 2, keepdims=False)
    w_other = flip(w_send.reshape(w_out.shape[0], 2 * width), 1)

    own = [hidden_in[c * step : (c + 1) * step] for c in range(n_chunk)]
    pair = flip(hidden_in, 1)
    pairs = [pair[c * step : (c + 1) * step] for c in range(n_chunk)]
    across = [flip(x, 2) for x in own]
    diagonal = [flip(x, 1) for x in across]

    block_end = jnp.sum(
        jnp.where(jnp.arange(n_dp)[:, None] <= jnp.arange(n_dp)[None, :], row_loads[0][:, None], 0), 0
    )
    row_ids = jnp.arange(rows, dtype=jnp.int32)
    dest_of = jnp.sum((block_end[:, None] <= row_ids[None, :]).astype(jnp.int32), 0)
    key_own = (dest_of * SEG_SPAN + seg_ids) * POS_SPAN + pos_ids
    key_all = lax.all_gather(key_own, "dp", axis=0)
    shard_of = me - jnp.arange(n_dp)
    key_k = key_all[shard_of % n_dp]
    doc_q = (key_own // POS_SPAN).reshape(-1, QUERY_BLOCK)
    doc_k = (key_k // POS_SPAN).reshape(n_dp, -1, KEY_BLOCK)
    first_q, last_q = doc_q[:, 0], doc_q[:, -1]
    first_k, last_k = doc_k[:, :, 0], doc_k[:, :, -1]
    begin = jnp.sum((last_k[None] < first_q[:, None, None]).astype(jnp.int32), 2)
    end = jnp.sum((first_k[None] <= last_q[:, None, None]).astype(jnp.int32), 2)
    end = jnp.where(shard_of[None, :] >= 0, end, 0)

    half = HEAD_WIDTH // 2
    inverse = ROPE_BASE ** (-(jnp.arange(half, dtype=jnp.float32) * 2.0) / HEAD_WIDTH)
    angles = pos_ids.astype(jnp.float32)[:, None] * inverse
    cosine, sine = jnp.cos(angles), jnp.sin(angles)
    cos = jnp.concatenate([cosine, cosine], 1)
    sin = jnp.concatenate([-sine, sine], 1)
    gain = attn_gain.astype(jnp.float32).reshape(-1, width)
    ids = jnp.stack([t, t ^ 1, t ^ 2, t ^ 3]).astype(jnp.int32)

    q_parts, kv_parts = [], [[] for _ in range(n_dp)]
    for c in range(n_chunk):
        span = slice(c * step, (c + 1) * step)
        q, kv = qkv(
            ids,
            (own[c], pairs[c], across[c], diagonal[c]),
            gain,
            w_query,
            key_matrix,
            value_matrix,
            cos[span],
            sin[span],
        )
        q_parts.append(q)
        kv_parts[0].append(kv)
        for d in range(1, n_dp):
            kv_parts[d].append(lax.ppermute(kv, "dp", [(i, i + d) for i in range(n_dp - d)]))

    order = prompt_order.reshape(rows, 1)
    heads = attend(
        begin,
        end,
        q_parts,
        [kv for parts in kv_parts for kv in parts],
        key_own.reshape(rows, 1),
        (key_own // POS_SPAN * POS_SPAN).reshape(rows, 1),
        key_k.reshape(-1, KEY_BLOCK),
        order,
    )
    heads_other = flip(heads, 1)
    far = jnp.stack([t ^ 2, 1 - t // 2]).astype(jnp.int32)
    near = jnp.stack([t, t // 2]).astype(jnp.int32)
    sent = [
        flip(project(far, heads, heads_other, w_out, w_other, width, j, n_part), 2)
        for j in range(n_part)
    ]
    kept = keep(near, order, hidden_in, heads, heads_other, w_out, w_other)
    final = final_gain.astype(jnp.float32).reshape(1, width)
    head = value_head.astype(jnp.float32).reshape(1, width)
    hidden, sums = None, []
    for j in range(n_part):
        hidden, part = finish(kept, sent[j], final, head, j, n_part, hidden)
        sums.append(part)
    square, product = lax.psum(jnp.concatenate(sums, 1), "tensor")
    return hidden, product * lax.rsqrt(square / MODEL_WIDTH + NORM_EPS)


def solution(mesh):
    return jax.shard_map(
        on_device,
        mesh=mesh,
        in_specs=(
            P(("parts", "dp"), "tensor"),
            P(("parts", "dp"), None),
            P(("parts", "dp")),
            P(("parts", "dp")),
            P(("parts", "dp"), None),
            P(),
            P(None, "tensor"),
            P(None, "tensor"),
            P(None, "tensor"),
            P("tensor", None),
            P("tensor"),
            P("tensor"),
        ),
        out_specs=(P(("parts", "dp"), "tensor"), P(("parts", "dp"))),
        check_vma=False,
    )
```

```python
import functools
import math

import jax
import jax.numpy as jnp
from jax import lax
from jax.experimental import pallas as pl
from jax.experimental.pallas import tpu as pltpu
from jax.sharding import PartitionSpec as P

MODEL_WIDTH = 4096
HEAD_WIDTH = 128
NORM_EPS = 1e-05
ROPE_BASE = 500000.0

SEG_SPAN = 64
POS_SPAN = 1024
POS_DIGIT = 128
DIGIT_ROWS = 16

QUERY_BLOCK = 128
KEY_BLOCK = 256
MASKED = -1e30

VMEM = pltpu.VMEM
EARLY_MIB = 16
TOKEN = jax.ShapeDtypeStruct((8, 128), jnp.float32)


def params(limit_mib):
    return pltpu.CompilerParams(vmem_limit_bytes=limit_mib * 2**20)


def cost(flops, bytes_accessed):
    return pl.CostEstimate(flops=flops, bytes_accessed=bytes_accessed, transcendentals=0)


def whole():
    return pl.BlockSpec(memory_space=VMEM)


def far_memory():
    return pl.BlockSpec(memory_space=pltpu.HBM)


def prep_kernel(loads, seg, pos, digits, cos, sin):
    lines, lanes = seg.shape
    row = lanes * lax.broadcasted_iota(jnp.int32, seg.shape, 0) + lax.broadcasted_iota(jnp.int32, seg.shape, 1)
    dest = jnp.zeros(seg.shape, jnp.int32)
    total = 0
    for e in range(loads.shape[1]):
        total = total + loads[0, e]
        dest += jnp.where(row >= total, 1, 0)
    low_pos = lax.bitwise_and(pos[...], POS_DIGIT - 1)
    high_pos = lax.shift_right_logical(pos[...], POS_DIGIT.bit_length() - 1)
    digits[...] = jnp.zeros(digits.shape, digits.dtype)
    for j, digit in enumerate((low_pos, high_pos, seg[...], dest)):
        line = jnp.concatenate([digit[i : i + 1, :] for i in range(lines)], 1)
        digits[j : j + 1, :] = line.astype(jnp.float32).astype(digits.dtype)
    at = pos[...].astype(jnp.float32)
    half = HEAD_WIDTH // 2
    lane = lax.broadcasted_iota(jnp.int32, (lanes, HEAD_WIDTH), 1)
    low = lane < half
    power = jnp.where(low, lane, lane - half).astype(jnp.float32)
    inverse = jnp.exp(power * (-2.0 * math.log(ROPE_BASE) / HEAD_WIDTH))
    for i in range(lines):
        column = jnp.broadcast_to(at[i : i + 1, :], (lanes, lanes)).T
        angle = column * inverse
        span = slice(i * lanes, (i + 1) * lanes)
        sine = jnp.sin(angle)
        cos[span, :] = jnp.cos(angle)
        sin[span, :] = jnp.where(low, -sine, sine)


def prep(row_loads, seg, pos):
    lines, lanes = seg.shape
    rows = lines * lanes
    table = jax.ShapeDtypeStruct((rows, HEAD_WIDTH), jnp.float32)
    return pl.pallas_call(
        prep_kernel,
        out_shape=(jax.ShapeDtypeStruct((DIGIT_ROWS, rows), jnp.bfloat16), table, table),
        in_specs=[pl.BlockSpec(memory_space=pltpu.SMEM), whole(), whole()],
        out_specs=(whole(), whole(), whole()),
        compiler_params=params(6),
        cost_estimate=cost(2 * 10**9, 4 * 10**7),
        name="prep",
    )(row_loads, seg, pos)


def gained(piece, gain, number):
    x = piece[...].astype(jnp.float32)
    width = x.shape[1]
    factor = gain[:, pl.ds(pl.multiple_of(number * width, width), width)].astype(jnp.float32)
    return jnp.sum(x * x, -1, keepdims=True), (x * factor).astype(jnp.bfloat16)


def weight_copies(weights, to, sem, ids, width):
    copies = []
    for i, number in enumerate(ids):
        at = 0
        rows = pl.ds(pl.multiple_of(number * width, width), width)
        for weight in weights:
            columns = pl.ds(at, weight.shape[1])
            copies.append(pltpu.make_async_copy(weight.at[rows, :], to.at[i, :, columns], sem.at[len(copies)]))
            at += weight.shape[1]
    return copies


def start(copies):
    for copy in copies:
        copy.start()


def wait(copies):
    for copy in copies:
        copy.wait()


def early_kernel(own, r0, r1, gain, wq, wk, wv, acc, squares, far_weights, token, held, sem):
    del token
    width = r0.shape[1]
    t = own[0]
    near = weight_copies((wq, wk, wv), held, sem.at[0], (t, lax.bitwise_xor(t, 1)), width)
    far = weight_copies(
        (wq, wk, wv), far_weights, sem.at[1], (lax.bitwise_xor(t, 2), lax.bitwise_xor(t, 3)), width
    )
    start(near)
    start(far)
    square0, x0 = gained(r0, gain, t)
    wait(near[:3])
    acc[...] = jnp.dot(x0, held[0], preferred_element_type=jnp.float32)
    square1, x1 = gained(r1, gain, lax.bitwise_xor(t, 1))
    wait(near[3:])
    acc[...] += jnp.dot(x1, held[1], preferred_element_type=jnp.float32)
    squares[...] = square0 + square1
    wait(far)


def early(own, r0, r1, gain, wq, wk, wv):
    rows, width = r0.shape
    columns = wq.shape[1] + wk.shape[1] + wv.shape[1]
    half = (2, width, columns)
    return pl.pallas_call(
        early_kernel,
        out_shape=(
            jax.ShapeDtypeStruct((rows, columns), jnp.float32),
            jax.ShapeDtypeStruct((rows, 1), jnp.float32),
            jax.ShapeDtypeStruct(half, jnp.bfloat16),
            TOKEN,
        ),
        in_specs=[pl.BlockSpec(memory_space=pltpu.SMEM)] + [whole()] * 3 + [far_memory()] * 3,
        out_specs=(whole(), whole(), whole(), far_memory()),
        scratch_shapes=[VMEM(half, jnp.bfloat16), pltpu.SemaphoreType.DMA((2, 6))],
        compiler_params=params(12),
        cost_estimate=cost(4 * rows * width * columns, 8 * width * columns),
        name="early",
    )(own, r0, r1, gain, wq, wk, wv)


def digit_lines(rows):
    return [(i, min(2 * HEAD_WIDTH, rows - i)) for i in range(0, rows, 2 * HEAD_WIDTH)]


def late_kernel(at, own, before, acc, squares, r2, r3, gain, weights, cos, sin, digits, q_out, kv_out, token):
    del before, token
    rows = r2.shape[0]
    span = slice(at, at + rows)
    square2, x2 = gained(r2, gain, lax.bitwise_xor(own[0], 2))
    total = acc[span, :] + jnp.dot(x2, weights[0], preferred_element_type=jnp.float32)
    square3, x3 = gained(r3, gain, lax.bitwise_xor(own[0], 3))
    total += jnp.dot(x3, weights[1], preferred_element_type=jnp.float32)
    total *= lax.rsqrt((squares[span, :] + square2 + square3) / MODEL_WIDTH + NORM_EPS)
    cosine, sine = cos[span, :], sin[span, :]
    n_head = q_out.shape[0]

    def rope(x):
        return (x * cosine + pltpu.roll(x, HEAD_WIDTH // 2, 1) * sine).astype(jnp.bfloat16)

    for h in range(n_head):
        q_out[h] = rope(total[:, h * HEAD_WIDTH : (h + 1) * HEAD_WIDTH])
    kv_out[:rows, :HEAD_WIDTH] = rope(total[:, n_head * HEAD_WIDTH : (n_head + 1) * HEAD_WIDTH])
    kv_out[:rows, HEAD_WIDTH:] = total[:, (n_head + 1) * HEAD_WIDTH :].astype(jnp.bfloat16)
    for i, (line, count) in enumerate(digit_lines(rows)):
        to = rows + i * DIGIT_ROWS
        kv_out[to : to + DIGIT_ROWS, :count] = digits[:, at + line : at + line + count]


def late(at, own, before, acc, squares, r2, r3, gain, weights, cos, sin, digits):
    rows, width = r2.shape
    columns = acc.shape[1]
    heads = columns // HEAD_WIDTH - 2
    return pl.pallas_call(
        functools.partial(late_kernel, at),
        out_shape=(
            jax.ShapeDtypeStruct((heads, rows, HEAD_WIDTH), jnp.bfloat16),
            jax.ShapeDtypeStruct((rows + DIGIT_ROWS * len(digit_lines(rows)), 2 * HEAD_WIDTH), jnp.bfloat16),
            TOKEN,
        ),
        in_specs=[pl.BlockSpec(memory_space=pltpu.SMEM), far_memory()] + [whole()] * 9,
        out_specs=(whole(), whole(), far_memory()),
        compiler_params=params(8),
        cost_estimate=cost(4 * rows * width * columns, 4 * width * columns),
        name="late",
    )(own, before, acc, squares, r2, r3, gain, weights, cos, sin, digits)


def pick_rows(order, x):
    rows = x.shape[0]
    pick = (order == lax.broadcasted_iota(jnp.int32, (rows, rows), 0)).astype(jnp.bfloat16)
    return lax.dot_general(pick, x, (((0,), (0,)), ((), ())), preferred_element_type=jnp.float32)


def attend_kernel(sizes, pieces, first, last, me, *refs):
    refs = list(refs)

    def take(count):
        taken = refs[:count]
        del refs[:count]
        return taken

    q_in = take(len(sizes))
    kv_in = take(len(pieces))
    if not first:
        m_in, l_in, acc_in, own_keys = take(4)
    if last:
        order, out, heads, m_s, l_s, acc_s = take(6)
    else:
        m_out, l_out, acc_out, own_keys_out, m_s, l_s, acc_s = take(7)
    q_all, kv_all, keys, keys_s, sem = refs
    n_head, rows, _ = q_all.shape
    n_query = rows // QUERY_BLOCK
    n_key = kv_all.shape[0] // KEY_BLOCK
    lanes = keys.shape[1]
    row = 0
    for (d, size), source in zip(pieces, kv_in, strict=True):
        for i, (line, count) in enumerate(digit_lines(size)):
            at = size + i * DIGIT_ROWS
            digit = source[at : at + DIGIT_ROWS, :count].astype(jnp.float32).astype(jnp.int32)
            doc = digit[3:4] * SEG_SPAN + digit[2:3]
            key = doc * POS_SPAN + digit[1:2] * POS_DIGIT + digit[0:1]
            key = jnp.where(d <= me[0], key, -1)
            for j in range(0, count, lanes):
                to = (row + line + j) // lanes
                keys[to : to + 1, :] = key[:, j : j + lanes]
        row += size
    own_line = row // lanes
    if first:
        own_line = 0
    else:
        keys[own_line : own_line + n_query, :] = own_keys[...]
    copy = pltpu.make_async_copy(keys, keys_s, sem)
    copy.start()
    if not last:
        own_keys_out[...] = keys[:n_query, :]
    for c, size in enumerate(sizes):
        at = sum(sizes[:c])
        q_all[:, at : at + size, :] = q_in[c][...]
    row = 0
    for (_, size), source in zip(pieces, kv_in, strict=True):
        kv_all[row : row + size, :] = source[:size, :]
        row += size
    copy.wait()
    scale = 1.4426950408889634 / HEAD_WIDTH**0.5
    stacked = n_head * QUERY_BLOCK
    lines = KEY_BLOCK // lanes

    def block(qb, _):
        at = pl.ds(pl.multiple_of(qb * QUERY_BLOCK, QUERY_BLOCK), QUERY_BLOCK)
        flat = pl.ds(pl.multiple_of(qb * stacked, stacked), stacked)
        q = q_all[:, at, :].reshape(stacked, HEAD_WIDTH)
        high = jnp.broadcast_to(keys[pl.ds(own_line + qb, 1), :], (QUERY_BLOCK, lanes)).T
        low = high - lax.bitwise_and(high, POS_SPAN - 1)
        high, low = (jnp.concatenate([x] * lines, 1) for x in (high, low))
        lowest = keys_s[own_line + qb, 0]
        lowest = lowest - lax.bitwise_and(lowest, POS_SPAN - 1)
        highest = lax.bitwise_or(keys_s[own_line + qb, lanes - 1], POS_SPAN - 1)
        if first:
            m_s[...] = jnp.full(m_s.shape, MASKED, jnp.float32)
            l_s[...] = jnp.zeros(l_s.shape, jnp.float32)
            acc_s[...] = jnp.zeros(acc_s.shape, jnp.float32)
        else:
            m_s[...] = m_in[flat, :]
            l_s[...] = l_in[flat, :]
            acc_s[...] = acc_in[flat, :]

        def keys_of(index, _):
            @pl.when((keys_s[index * lines + lines - 1, lanes - 1] >= lowest) & (keys_s[index * lines, 0] <= highest))
            def _():
                span = pl.ds(pl.multiple_of(index * KEY_BLOCK, KEY_BLOCK), KEY_BLOCK)
                k = kv_all[span, :HEAD_WIDTH]
                v = kv_all[span, HEAD_WIDTH:]
                s = lax.dot_general(q, k, (((1,), (1,)), ((), ())), preferred_element_type=jnp.float32)
                ids = jnp.concatenate([keys[pl.ds(index * lines + i, 1), :] for i in range(lines)], 1)
                allowed = (ids <= high) & (ids >= low)
                s = jnp.where(allowed[None], (s * scale).reshape(n_head, QUERY_BLOCK, KEY_BLOCK), MASKED)
                s = s.reshape(stacked, KEY_BLOCK)
                m_old = m_s[...]
                m_new = jnp.maximum(m_old, jnp.max(s, -1, keepdims=True))
                alpha = jnp.exp2(m_old - m_new)
                p = [
                    jnp.exp2(s[:, i : i + HEAD_WIDTH] - m_new) for i in range(0, KEY_BLOCK, HEAD_WIDTH)
                ]
                m_s[...] = m_new
                l_s[...] = l_s[...] * alpha + functools.reduce(jnp.add, p)
                p = jnp.concatenate(p, 1).astype(jnp.bfloat16)
                acc_s[...] = acc_s[...] * alpha + jnp.dot(p, v, preferred_element_type=jnp.float32)

            return 0

        lax.fori_loop(0, n_key, keys_of, 0)
        if last:
            done = (acc_s[...] / jnp.sum(l_s[...], -1, keepdims=True)).astype(jnp.bfloat16)
            for h in range(n_head):
                heads[at, h * HEAD_WIDTH : (h + 1) * HEAD_WIDTH] = done[h * QUERY_BLOCK : (h + 1) * QUERY_BLOCK]
        else:
            m_out[flat, :] = m_s[...]
            l_out[flat, :] = l_s[...]
            acc_out[flat, :] = acc_s[...]
        return 0

    lax.fori_loop(0, n_query, block, 0)
    if last:
        out[...] = pick_rows(order[...], heads[...]).astype(jnp.bfloat16)


def attend(me, q_parts, pieces, kv_parts, state, order):
    first, last = state is None, order is not None
    n_head = q_parts[0].shape[0]
    sizes = tuple(q.shape[1] for q in q_parts)
    rows = sum(sizes)
    n_key = sum(size for _, size in pieces)
    n_query = rows // QUERY_BLOCK
    stacked = n_head * QUERY_BLOCK
    key_lines = (n_key // QUERY_BLOCK + (0 if first else n_query), QUERY_BLOCK)
    running = jax.ShapeDtypeStruct((n_head * rows, HEAD_WIDTH), jnp.float32)
    inputs = [*q_parts, *kv_parts] + ([] if first else list(state)) + ([order] if last else [])
    if last:
        out_shape = jax.ShapeDtypeStruct((rows, n_head * HEAD_WIDTH), jnp.bfloat16)
        out_specs = whole()
    else:
        out_shape = (running,) * 3 + (jax.ShapeDtypeStruct((n_query, QUERY_BLOCK), jnp.int32),)
        out_specs = (whole(),) * 4
    return pl.pallas_call(
        functools.partial(attend_kernel, sizes, tuple(pieces), first, last),
        out_shape=out_shape,
        in_specs=[pl.BlockSpec(memory_space=pltpu.SMEM)] + [whole()] * len(inputs),
        out_specs=out_specs,
        scratch_shapes=([VMEM((rows, n_head * HEAD_WIDTH), jnp.bfloat16)] if last else [])
        + [VMEM((stacked, HEAD_WIDTH), jnp.float32)] * 3
        + [
            VMEM((n_head, rows, HEAD_WIDTH), jnp.bfloat16),
            VMEM((n_key, 2 * HEAD_WIDTH), jnp.bfloat16),
            VMEM(key_lines, jnp.int32),
            pltpu.SMEM(key_lines, jnp.int32),
            pltpu.SemaphoreType.DMA(()),
        ],
        compiler_params=params(12 + n_key // 512),
        cost_estimate=cost(4 * rows * n_key * n_head * HEAD_WIDTH, 4 * rows * n_head * HEAD_WIDTH),
        name="attend",
    )(me, *inputs)


def columns_kernel(own, w_out, token_in, near, far, send_near, send_far, token, sem):
    del token_in, token
    width = near.shape[1]
    copies = []
    for i, (bits, to) in enumerate(((3, send_far), (1, send_near), (2, far), (0, near))):
        at = pl.ds(pl.multiple_of(lax.bitwise_xor(own[0], bits) * width, width), width)
        copies.append(pltpu.make_async_copy(w_out.at[:, at], to, sem.at[i]))
    start(copies)
    wait(copies)


def columns(own, w_out, token, width):
    block = jax.ShapeDtypeStruct((w_out.shape[0], width), w_out.dtype)
    return pl.pallas_call(
        columns_kernel,
        out_shape=(block,) * 4 + (TOKEN,),
        in_specs=[pl.BlockSpec(memory_space=pltpu.SMEM), far_memory(), far_memory()],
        out_specs=(whole(),) * 4 + (far_memory(),),
        scratch_shapes=[pltpu.SemaphoreType.DMA((4,))],
        compiler_params=params(6),
        cost_estimate=cost(1, 4 * w_out.size),
        name="columns",
    )(own, w_out, token)


def project_kernel(h0, h1, w0, w1, out):
    total = jnp.dot(h0[...], w0[...], preferred_element_type=jnp.float32)
    total += jnp.dot(h1[...], w1[...], preferred_element_type=jnp.float32)
    out[...] = total.astype(out.dtype)


def project(h0, h1, w0, w1, part, n_part):
    rows, depth = h0.shape
    width = w0.shape[1]
    step = rows // n_part
    return pl.pallas_call(
        project_kernel,
        grid=(1,),
        in_specs=[
            pl.BlockSpec((step, depth), lambda i: (part, 0)),
            pl.BlockSpec((step, depth), lambda i: (part, 0)),
            pl.BlockSpec((depth, width), lambda i: (0, 0)),
            pl.BlockSpec((depth, width), lambda i: (0, 0)),
        ],
        out_specs=pl.BlockSpec((step, width), lambda i: (0, 0)),
        out_shape=jax.ShapeDtypeStruct((step, width), jnp.bfloat16),
        compiler_params=params(10),
        cost_estimate=cost(4 * step * depth * width, 4 * depth * width),
        name="project",
    )(h0, h1, w0, w1)


def keep_kernel(order, own, h0, h1, w0, w1, out):
    total = jnp.dot(h0[...], w0[...], preferred_element_type=jnp.float32)
    total += jnp.dot(h1[...], w1[...], preferred_element_type=jnp.float32)
    out[...] = total + pick_rows(order[...], own[...])


def keep(order, own, h0, h1, w0, w1):
    rows, width = own.shape
    depth = h0.shape[1]
    return pl.pallas_call(
        keep_kernel,
        out_shape=jax.ShapeDtypeStruct((rows, width), jnp.float32),
        in_specs=[whole()] * 6,
        out_specs=whole(),
        compiler_params=params(12),
        cost_estimate=cost(2 * rows * (2 * depth + rows) * width, 4 * depth * width + 6 * rows * width),
        name="keep",
    )(order, own, h0, h1, w0, w1)


def finish_kernel(kept, received, gain, head, *refs):
    hidden_out, sums = refs[-2:]
    hidden = (kept[...] + received[...].astype(jnp.float32)).astype(jnp.bfloat16)
    hidden_out[...] = hidden
    x = hidden.astype(jnp.float32)
    weighted = x * (gain[...] * head[...])
    squared = x * x
    for i, terms in enumerate((squared, weighted)):
        lanes = functools.reduce(
            jnp.add, [terms[:, j : j + 128] for j in range(0, terms.shape[1], 128)]
        )
        sums[i : i + 1, :] = jnp.sum(lanes.T, 0, keepdims=True)


def finish(kept, received, gain, head, part, n_part, hidden):
    rows, width = kept.shape
    step = rows // n_part
    specs = [
        pl.BlockSpec((step, width), lambda i: (part, 0)),
        pl.BlockSpec((step, width), lambda i: (0, 0)),
        pl.BlockSpec((1, width), lambda i: (0, 0)),
        pl.BlockSpec((1, width), lambda i: (0, 0)),
    ]
    args = [kept, received, gain, head]
    aliases = {}
    if hidden is not None:
        specs.append(pl.BlockSpec(memory_space=pl.ANY))
        args.append(hidden)
        aliases = {4: 0}
    return pl.pallas_call(
        finish_kernel,
        grid=(1,),
        in_specs=specs,
        out_specs=(
            pl.BlockSpec((step, width), lambda i: (part, 0)),
            pl.BlockSpec((2, step), lambda i: (0, 0)),
        ),
        out_shape=(
            jax.ShapeDtypeStruct((rows, width), jnp.bfloat16),
            jax.ShapeDtypeStruct((2, step), jnp.float32),
        ),
        input_output_aliases=aliases,
        compiler_params=params(8),
        cost_estimate=cost(6 * step * width, 8 * step * width),
        name="finish",
    )(*args)


def flip(x, bit):
    count = lax.axis_size("tensor")
    return lax.ppermute(x, "tensor", [(i, i ^ bit) for i in range(count)])


def chunk_sizes(rows, n_dp):
    if n_dp > 8 or rows % 128:
        return (rows,)
    return (rows // 2, rows // 2)


def on_device(
    hidden_in,
    row_loads,
    seg_ids,
    pos_ids,
    prompt_order,
    attn_gain,
    w_query,
    key_matrix,
    value_matrix,
    w_out,
    final_gain,
    value_head,
):
    n_dp = lax.axis_size("dp")
    me = lax.axis_index("dp")
    t = lax.axis_index("tensor")
    rows, width = hidden_in.shape
    sizes = chunk_sizes(rows, n_dp)
    n_part = 2

    own = [hidden_in[sum(sizes[:c]) : sum(sizes[: c + 1])] for c in range(len(sizes))]
    across = [flip(x, 2) for x in own]
    pair = flip(hidden_in, 1)

    lines = rows // QUERY_BLOCK
    digits, cos, sin = prep(
        row_loads, seg_ids.reshape(lines, QUERY_BLOCK), pos_ids.reshape(lines, QUERY_BLOCK)
    )
    gain = attn_gain.reshape(1, -1)
    t_own = t.astype(jnp.int32).reshape(1)
    acc, squares, far_weights, token = early(
        t_own, hidden_in, pair, gain, w_query, key_matrix, value_matrix
    )

    q_parts, kv_parts = [], [[] for _ in range(n_dp)]
    for c in range(len(sizes)):
        if c > 0:
            for d in range(1, n_dp):
                kv_parts[d][-1], token = lax.optimization_barrier((kv_parts[d][-1], token))
        received, token = lax.optimization_barrier((across[c], token))
        diagonal = flip(received, 1)
        q, kv, token = late(
            sum(sizes[:c]), t_own, token, acc, squares, received, diagonal, gain, far_weights, cos, sin, digits
        )
        q_parts.append(q)
        kv_parts[0].append(kv)
        for d in range(1, n_dp):
            kv_parts[d].append(lax.ppermute(kv, "dp", [(i, (i + d) % n_dp) for i in range(n_dp)]))
        if c == 0:
            near, far, send_near, send_far, token = columns(t_own, w_out, token, width)
            near_other, far_other = flip(send_near, 1), flip(send_far, 1)

    order = prompt_order.reshape(1, rows)
    me_own = me.astype(jnp.int32).reshape(1)
    numbers = range(len(sizes))
    soon = [(0, c) for c in numbers] + [(d, c) for d in range(1, n_dp) for c in numbers[:-1]]
    then = [(d, numbers[-1]) for d in range(1, n_dp)]
    if len(sizes) == 1:
        soon, then = soon + then, []
    state = None
    for some in (soon, then):
        if some:
            pieces = [(d, sizes[c]) for d, c in some]
            last = some is then or not then
            state = attend(
                me_own, q_parts, pieces, [kv_parts[d][c] for d, c in some], state, order if last else None
            )
    heads = state
    heads_other = flip(heads, 1)
    sent = [
        flip(project(heads, heads_other, far, far_other, j, n_part), 2) for j in range(n_part)
    ]
    kept = keep(order, hidden_in, heads, heads_other, near, near_other)
    final = final_gain.astype(jnp.float32).reshape(1, width)
    head = value_head.astype(jnp.float32).reshape(1, width)
    hidden, sums = None, []
    for j in range(n_part):
        hidden, part = finish(kept, sent[j], final, head, j, n_part, hidden)
        sums.append(part)
    square, product = lax.psum(jnp.concatenate(sums, 1), "tensor")
    return hidden, product * lax.rsqrt(square / MODEL_WIDTH + NORM_EPS)


def solution(mesh):
    return jax.shard_map(
        on_device,
        mesh=mesh,
        in_specs=(
            P(("parts", "dp"), "tensor"),
            P(("parts", "dp"), None),
            P(("parts", "dp")),
            P(("parts", "dp")),
            P(("parts", "dp"), None),
            P(),
            P(None, "tensor"),
            P(None, "tensor"),
            P(None, "tensor"),
            P("tensor", None),
            P("tensor"),
            P("tensor"),
        ),
        out_specs=(P(("parts", "dp"), "tensor"), P(("parts", "dp"))),
        check_vma=False,
    )
```

```python
import functools
import math

import jax
import jax.numpy as jnp
from jax import lax
from jax.experimental import pallas as pl
from jax.experimental.pallas import tpu as pltpu
from jax.sharding import PartitionSpec as P

MODEL_WIDTH = 4096
HEAD_WIDTH = 128
NORM_EPS = 1e-05
ROPE_BASE = 500000.0

SEG_SPAN = 64
POS_SPAN = 1024
POS_DIGIT = 128
DIGIT_ROWS = 16
N_PART = 2

QUERY_BLOCK = 128
KEY_BLOCK = 256
MASKED = -1e30

VMEM = pltpu.VMEM
EARLY_MIB = 16
TOKEN = jax.ShapeDtypeStruct((8, 128), jnp.float32)


def params(limit_mib):
    return pltpu.CompilerParams(vmem_limit_bytes=limit_mib * 2**20)


def cost(flops, bytes_accessed):
    return pl.CostEstimate(flops=flops, bytes_accessed=bytes_accessed, transcendentals=0)


def whole():
    return pl.BlockSpec(memory_space=VMEM)


def far_memory():
    return pl.BlockSpec(memory_space=pltpu.HBM)


def prep_kernel(loads, seg, pos, digits, cos, sin):
    lines, lanes = seg.shape
    row = lanes * lax.broadcasted_iota(jnp.int32, seg.shape, 0) + lax.broadcasted_iota(jnp.int32, seg.shape, 1)
    dest = jnp.zeros(seg.shape, jnp.int32)
    total = 0
    for e in range(loads.shape[1]):
        total = total + loads[0, e]
        dest += jnp.where(row >= total, 1, 0)
    low_pos = lax.bitwise_and(pos[...], POS_DIGIT - 1)
    high_pos = lax.shift_right_logical(pos[...], POS_DIGIT.bit_length() - 1)
    digits[...] = jnp.zeros(digits.shape, digits.dtype)
    for j, digit in enumerate((low_pos, high_pos, seg[...], dest)):
        line = jnp.concatenate([digit[i : i + 1, :] for i in range(lines)], 1)
        digits[j : j + 1, :] = line.astype(jnp.float32).astype(digits.dtype)
    at = pos[...].astype(jnp.float32)
    half = HEAD_WIDTH // 2
    lane = lax.broadcasted_iota(jnp.int32, (lanes, HEAD_WIDTH), 1)
    low = lane < half
    power = jnp.where(low, lane, lane - half).astype(jnp.float32)
    inverse = jnp.exp(power * (-2.0 * math.log(ROPE_BASE) / HEAD_WIDTH))
    for i in range(lines):
        column = jnp.broadcast_to(at[i : i + 1, :], (lanes, lanes)).T
        angle = column * inverse
        span = slice(i * lanes, (i + 1) * lanes)
        sine = jnp.sin(angle)
        cos[span, :] = jnp.cos(angle)
        sin[span, :] = jnp.where(low, -sine, sine)


def prep(row_loads, seg, pos):
    lines, lanes = seg.shape
    rows = lines * lanes
    table = jax.ShapeDtypeStruct((rows, HEAD_WIDTH), jnp.float32)
    return pl.pallas_call(
        prep_kernel,
        out_shape=(jax.ShapeDtypeStruct((DIGIT_ROWS, rows), jnp.bfloat16), table, table),
        in_specs=[pl.BlockSpec(memory_space=pltpu.SMEM), whole(), whole()],
        out_specs=(whole(), whole(), whole()),
        compiler_params=params(6),
        cost_estimate=cost(2 * 10**9, 4 * 10**7),
        name="prep",
    )(row_loads, seg, pos)


def gained(piece, gain, number):
    x = piece[...].astype(jnp.float32)
    width = x.shape[1]
    factor = gain[:, pl.ds(pl.multiple_of(number * width, width), width)].astype(jnp.float32)
    return jnp.sum(x * x, -1, keepdims=True), (x * factor).astype(jnp.bfloat16)


def weight_copies(weights, to, sem, ids, width):
    copies = []
    for i, number in enumerate(ids):
        at = 0
        rows = pl.ds(pl.multiple_of(number * width, width), width)
        for weight in weights:
            columns = pl.ds(at, weight.shape[1])
            copies.append(pltpu.make_async_copy(weight.at[rows, :], to.at[i, :, columns], sem.at[len(copies)]))
            at += weight.shape[1]
    return copies


def start(copies):
    for copy in copies:
        copy.start()


def wait(copies):
    for copy in copies:
        copy.wait()


def early_kernel(own, r0, r1, gain, wq, wk, wv, acc, squares, far_weights, token, held, sem):
    del token
    width = r0.shape[1]
    t = own[0]
    near = weight_copies((wq, wk, wv), held, sem.at[0], (t, lax.bitwise_xor(t, 1)), width)
    far = weight_copies(
        (wq, wk, wv), far_weights, sem.at[1], (lax.bitwise_xor(t, 2), lax.bitwise_xor(t, 3)), width
    )
    start(near)
    start(far)
    square0, x0 = gained(r0, gain, t)
    wait(near[:3])
    acc[...] = jnp.dot(x0, held[0], preferred_element_type=jnp.float32)
    square1, x1 = gained(r1, gain, lax.bitwise_xor(t, 1))
    wait(near[3:])
    acc[...] += jnp.dot(x1, held[1], preferred_element_type=jnp.float32)
    squares[...] = square0 + square1
    wait(far)


def early(own, r0, r1, gain, wq, wk, wv):
    rows, width = r0.shape
    columns = wq.shape[1] + wk.shape[1] + wv.shape[1]
    half = (2, width, columns)
    return pl.pallas_call(
        early_kernel,
        out_shape=(
            jax.ShapeDtypeStruct((rows, columns), jnp.float32),
            jax.ShapeDtypeStruct((rows, 1), jnp.float32),
            jax.ShapeDtypeStruct(half, jnp.bfloat16),
            TOKEN,
        ),
        in_specs=[pl.BlockSpec(memory_space=pltpu.SMEM)] + [whole()] * 3 + [far_memory()] * 3,
        out_specs=(whole(), whole(), whole(), far_memory()),
        scratch_shapes=[VMEM(half, jnp.bfloat16), pltpu.SemaphoreType.DMA((2, 6))],
        compiler_params=params(12),
        cost_estimate=cost(4 * rows * width * columns, 8 * width * columns),
        name="early",
    )(own, r0, r1, gain, wq, wk, wv)


def digit_lines(rows):
    return [(i, min(2 * HEAD_WIDTH, rows - i)) for i in range(0, rows, 2 * HEAD_WIDTH)]


def keys_of(digits, back, own):
    digit = digits.astype(jnp.float32).astype(jnp.int32)
    doc = digit[3:4] * SEG_SPAN + digit[2:3]
    key = doc * POS_SPAN + digit[1:2] * POS_DIGIT + digit[0:1]
    return jnp.where(back <= own[2], key, -1)


def unpack(pieces, sources, own, kv_all, keys):
    lanes = keys.shape[1]
    row = 0
    for (back, size), source in zip(pieces, sources, strict=True):
        kv_all[row : row + size, :] = source[:size, :]
        for i, (line, count) in enumerate(digit_lines(size)):
            at = size + i * DIGIT_ROWS
            key = keys_of(source[at : at + DIGIT_ROWS, :count], back, own)
            for j in range(0, count, lanes):
                to = (row + line + j) // lanes
                keys[to : to + 1, :] = key[:, j : j + lanes]
        row += size


def late_kernel(at, pieces, own, before, acc, squares, r2, r3, gain, weights, cos, sin, digits, *refs):
    del before
    refs = list(refs)
    rows = r2.shape[0]
    n_old = sum(1 for back, _ in pieces if back == 0)
    q_old, kv_old = refs[:n_old], refs[n_old : n_old + len(pieces)]
    q_out, kv_out, *outs = refs[n_old + len(pieces) :]
    span = slice(at, at + rows)
    square2, x2 = gained(r2, gain, lax.bitwise_xor(own[0], 2))
    total = acc[span, :] + jnp.dot(x2, weights[0], preferred_element_type=jnp.float32)
    square3, x3 = gained(r3, gain, lax.bitwise_xor(own[0], 3))
    total += jnp.dot(x3, weights[1], preferred_element_type=jnp.float32)
    total *= lax.rsqrt((squares[span, :] + square2 + square3) / MODEL_WIDTH + NORM_EPS)
    cosine, sine = cos[span, :], sin[span, :]
    n_head = q_out.shape[0]

    def rope(x):
        return (x * cosine + pltpu.roll(x, HEAD_WIDTH // 2, 1) * sine).astype(jnp.bfloat16)

    here = slice(at, at + rows) if q_out.shape[1] > rows else slice(0, rows)
    for h in range(n_head):
        q_out[h, here, :] = rope(total[:, h * HEAD_WIDTH : (h + 1) * HEAD_WIDTH])
    kv_out[:rows, :HEAD_WIDTH] = rope(total[:, n_head * HEAD_WIDTH : (n_head + 1) * HEAD_WIDTH])
    kv_out[:rows, HEAD_WIDTH:] = total[:, (n_head + 1) * HEAD_WIDTH :].astype(jnp.bfloat16)
    for i, (line, count) in enumerate(digit_lines(rows)):
        to = rows + i * DIGIT_ROWS
        kv_out[to : to + DIGIT_ROWS, :count] = digits[:, at + line : at + line + count]
    if len(outs) > 1:
        kv_all, keys, _ = outs
        row = 0
        for q in q_old:
            q_out[:, row : row + q.shape[1], :] = q[...]
            row += q.shape[1]
        sources = [*kv_old[:n_old], kv_out, *kv_old[n_old:]]
        unpack([*pieces[:n_old], (0, rows), *pieces[n_old:]], sources, own, kv_all, keys)


def late(at, own, before, acc, squares, r2, r3, gain, weights, cos, sin, digits, last, q_old, pieces, kv_old):
    rows, width = r2.shape
    columns = acc.shape[1]
    heads = columns // HEAD_WIDTH - 2
    n_key = rows + sum(size for _, size in pieces)
    more, specs = (), ()
    if last:
        more = (
            jax.ShapeDtypeStruct((n_key, 2 * HEAD_WIDTH), jnp.bfloat16),
            jax.ShapeDtypeStruct((n_key // QUERY_BLOCK, QUERY_BLOCK), jnp.int32),
        )
        specs = (whole(), whole())
    return pl.pallas_call(
        functools.partial(late_kernel, at, tuple(pieces)),
        out_shape=(
            jax.ShapeDtypeStruct((heads, at + rows if last else rows, HEAD_WIDTH), jnp.bfloat16),
            jax.ShapeDtypeStruct((rows + DIGIT_ROWS * len(digit_lines(rows)), 2 * HEAD_WIDTH), jnp.bfloat16),
            *more,
            TOKEN,
        ),
        in_specs=[pl.BlockSpec(memory_space=pltpu.SMEM), far_memory()]
        + [whole()] * (9 + len(q_old) + len(kv_old)),
        out_specs=(whole(), whole(), *specs, far_memory()),
        compiler_params=params(10),
        cost_estimate=cost(4 * rows * width * columns, 4 * width * columns),
        name="late",
    )(own, before, acc, squares, r2, r3, gain, weights, cos, sin, digits, *q_old, *kv_old)


def pick_rows(order, x):
    rows = x.shape[0]
    pick = (order == lax.broadcasted_iota(jnp.int32, (rows, rows), 0)).astype(jnp.bfloat16)
    return lax.dot_general(pick, x, (((0,), (0,)), ((), ())), preferred_element_type=jnp.float32)


def attend_kernel(pieces, last, own, q_all, *refs):
    refs = list(refs)

    def take(count):
        taken = refs[:count]
        del refs[:count]
        return taken

    n_head, rows, _ = q_all.shape
    n_query = rows // QUERY_BLOCK
    if last:
        m_in, l_in, acc_in, own_keys = take(4)
        kv_in = take(len(pieces))
        _, order, out, *parts = take(3 + N_PART)
        heads, kv_all, keys = take(3)
        unpack(pieces, kv_in, own, kv_all, keys)
        own_line = kv_all.shape[0] // QUERY_BLOCK
        keys[own_line : own_line + n_query, :] = own_keys[:n_query, :]
    else:
        kv_all, keys, m_out, l_out, acc_out, _ = take(6)
        own_line = 0
    m_s, l_s, acc_s, keys_s, sem = refs
    n_key = kv_all.shape[0] // KEY_BLOCK
    lanes = keys.shape[1]
    copy = pltpu.make_async_copy(keys, keys_s, sem)
    copy.start()
    copy.wait()
    scale = 1.4426950408889634 / HEAD_WIDTH**0.5
    stacked = n_head * QUERY_BLOCK
    lines = KEY_BLOCK // lanes

    def block(qb, _):
        at = pl.ds(pl.multiple_of(qb * QUERY_BLOCK, QUERY_BLOCK), QUERY_BLOCK)
        flat = pl.ds(pl.multiple_of(qb * stacked, stacked), stacked)
        q = q_all[:, at, :].reshape(stacked, HEAD_WIDTH)
        high = jnp.broadcast_to(keys[pl.ds(own_line + qb, 1), :], (QUERY_BLOCK, lanes)).T
        low = high - lax.bitwise_and(high, POS_SPAN - 1)
        high, low = (jnp.concatenate([x] * lines, 1) for x in (high, low))
        lowest = keys_s[own_line + qb, 0]
        lowest = lowest - lax.bitwise_and(lowest, POS_SPAN - 1)
        highest = lax.bitwise_or(keys_s[own_line + qb, lanes - 1], POS_SPAN - 1)
        if not last:
            m_s[...] = jnp.full(m_s.shape, MASKED, jnp.float32)
            l_s[...] = jnp.zeros(l_s.shape, jnp.float32)
            acc_s[...] = jnp.zeros(acc_s.shape, jnp.float32)
        else:
            m_s[...] = m_in[flat, :]
            l_s[...] = l_in[flat, :]
            acc_s[...] = acc_in[flat, :]

        def some_keys(index, _):
            @pl.when((keys_s[index * lines + lines - 1, lanes - 1] >= lowest) & (keys_s[index * lines, 0] <= highest))
            def _():
                span = pl.ds(pl.multiple_of(index * KEY_BLOCK, KEY_BLOCK), KEY_BLOCK)
                k = kv_all[span, :HEAD_WIDTH]
                v = kv_all[span, HEAD_WIDTH:]
                s = lax.dot_general(q, k, (((1,), (1,)), ((), ())), preferred_element_type=jnp.float32)
                ids = jnp.concatenate([keys[pl.ds(index * lines + i, 1), :] for i in range(lines)], 1)
                allowed = (ids <= high) & (ids >= low)
                s = jnp.where(allowed[None], (s * scale).reshape(n_head, QUERY_BLOCK, KEY_BLOCK), MASKED)
                s = s.reshape(stacked, KEY_BLOCK)
                m_old = m_s[...]
                m_new = jnp.maximum(m_old, jnp.max(s, -1, keepdims=True))
                alpha = jnp.exp2(m_old - m_new)
                p = [
                    jnp.exp2(s[:, i : i + HEAD_WIDTH] - m_new) for i in range(0, KEY_BLOCK, HEAD_WIDTH)
                ]
                m_s[...] = m_new
                l_s[...] = l_s[...] * alpha + functools.reduce(jnp.add, p)
                p = jnp.concatenate(p, 1).astype(jnp.bfloat16)
                acc_s[...] = acc_s[...] * alpha + jnp.dot(p, v, preferred_element_type=jnp.float32)

            return 0

        lax.fori_loop(0, n_key, some_keys, 0)
        if last:
            done = (acc_s[...] / jnp.sum(l_s[...], -1, keepdims=True)).astype(jnp.bfloat16)
            for h in range(n_head):
                heads[at, h * HEAD_WIDTH : (h + 1) * HEAD_WIDTH] = done[h * QUERY_BLOCK : (h + 1) * QUERY_BLOCK]
        else:
            m_out[flat, :] = m_s[...]
            l_out[flat, :] = l_s[...]
            acc_out[flat, :] = acc_s[...]
        return 0

    lax.fori_loop(0, n_query, block, 0)
    if last:
        picked = pick_rows(order[...], heads[...]).astype(jnp.bfloat16)
        out[...] = picked
        for i, part in enumerate(parts):
            part[...] = picked[i * part.shape[0] : (i + 1) * part.shape[0], :]


def attend(own, q_all, kv_all, keys):
    n_head, rows, _ = q_all.shape
    stacked = n_head * QUERY_BLOCK
    n_key = kv_all.shape[0]
    running = jax.ShapeDtypeStruct((n_head * rows, HEAD_WIDTH), jnp.float32)
    return pl.pallas_call(
        functools.partial(attend_kernel, (), False),
        out_shape=(running,) * 3 + (TOKEN,),
        in_specs=[pl.BlockSpec(memory_space=pltpu.SMEM)] + [whole()] * 3,
        out_specs=(whole(),) * 3 + (far_memory(),),
        scratch_shapes=[VMEM((stacked, HEAD_WIDTH), jnp.float32)] * 3
        + [pltpu.SMEM(keys.shape, jnp.int32), pltpu.SemaphoreType.DMA(())],
        compiler_params=params(12),
        cost_estimate=cost(4 * rows * n_key * n_head * HEAD_WIDTH, 4 * rows * n_head * HEAD_WIDTH),
        name="attend",
    )(own, q_all, kv_all, keys)


def attend_rest(own, q_all, state, own_keys, pieces, kv_parts, token, order):
    n_head, rows, _ = q_all.shape
    stacked = n_head * QUERY_BLOCK
    n_key = sum(size for _, size in pieces)
    key_lines = ((n_key + rows) // QUERY_BLOCK, QUERY_BLOCK)
    return pl.pallas_call(
        functools.partial(attend_kernel, tuple(pieces), True),
        out_shape=tuple(
            jax.ShapeDtypeStruct((size, n_head * HEAD_WIDTH), jnp.bfloat16)
            for size in [rows] + [rows // N_PART] * N_PART
        ),
        in_specs=[pl.BlockSpec(memory_space=pltpu.SMEM)]
        + [whole()] * (5 + len(pieces))
        + [far_memory(), whole()],
        out_specs=(whole(),) * (1 + N_PART),
        scratch_shapes=[
            VMEM((rows, n_head * HEAD_WIDTH), jnp.bfloat16),
            VMEM((n_key, 2 * HEAD_WIDTH), jnp.bfloat16),
            VMEM(key_lines, jnp.int32),
        ]
        + [VMEM((stacked, HEAD_WIDTH), jnp.float32)] * 3
        + [pltpu.SMEM(key_lines, jnp.int32), pltpu.SemaphoreType.DMA(())],
        compiler_params=params(12 + n_key // 512),
        cost_estimate=cost(4 * rows * n_key * n_head * HEAD_WIDTH, 4 * rows * n_head * HEAD_WIDTH),
        name="attend_rest",
    )(own, q_all, *state, own_keys, *kv_parts, token, order)


def columns_kernel(own, w_out, token_in, near, send_near, far, beside, token, sem):
    del token_in, token
    depth, width = near.shape
    half = depth // 2
    copies = []
    for bits, first, to in (
        (2, own[1] * half, far),
        (3, own[1] * half, beside),
        (1, 0, send_near),
        (0, 0, near),
    ):
        rows = pl.ds(pl.multiple_of(first, half), to.shape[0])
        at = pl.ds(pl.multiple_of(lax.bitwise_xor(own[0], bits) * width, width), width)
        copies.append(pltpu.make_async_copy(w_out.at[rows, at], to, sem.at[len(copies)]))
    start(copies)
    wait(copies)


def columns(own, w_out, token, width):
    rows = w_out.shape[0]
    blocks = [jax.ShapeDtypeStruct((size, width), w_out.dtype) for size in (rows, rows, rows // 2, rows // 2)]
    return pl.pallas_call(
        columns_kernel,
        out_shape=(*blocks, TOKEN),
        in_specs=[pl.BlockSpec(memory_space=pltpu.SMEM), far_memory(), far_memory()],
        out_specs=(whole(),) * 4 + (far_memory(),),
        scratch_shapes=[pltpu.SemaphoreType.DMA((5,))],
        compiler_params=params(6),
        cost_estimate=cost(1, 4 * w_out.size),
        name="columns",
    )(own, w_out, token)


def keep_kernel(order, own, h0, h1, w0, w1, out, token):
    del token
    total = jnp.dot(h0[...], w0[...], preferred_element_type=jnp.float32)
    total += jnp.dot(h1[...], w1[...], preferred_element_type=jnp.float32)
    out[...] = total + pick_rows(order[...], own[...])


def keep(order, own, h0, h1, w0, w1):
    rows, width = own.shape
    depth = h0.shape[1]
    return pl.pallas_call(
        keep_kernel,
        out_shape=(jax.ShapeDtypeStruct((rows, width), jnp.float32), TOKEN),
        in_specs=[whole()] * 6,
        out_specs=(whole(), far_memory()),
        compiler_params=params(12),
        cost_estimate=cost(2 * rows * (2 * depth + rows) * width, 4 * depth * width + 6 * rows * width),
        name="keep",
    )(order, own, h0, h1, w0, w1)


def finish_kernel(own, kept, h2, h3, gain, head, *refs):
    (w2, other2, w3, other3), (hidden_out, sums) = refs[:4], refs[-2:]
    half = w2.shape[0]
    mine = pl.ds(pl.multiple_of(own[1] * half, half), half)
    others = pl.ds(pl.multiple_of((1 - own[1]) * half, half), half)
    total = kept[...]
    for h, columns, weight in ((h2, mine, w2), (h3, mine, w3), (h2, others, other2), (h3, others, other3)):
        total += jnp.dot(h[:, columns], weight[...], preferred_element_type=jnp.float32)
    hidden = total.astype(jnp.bfloat16)
    hidden_out[...] = hidden
    x = hidden.astype(jnp.float32)
    weighted = x * (gain[...] * head[...])
    squared = x * x
    for i, terms in enumerate((squared, weighted)):
        lanes = functools.reduce(
            jnp.add, [terms[:, j : j + 128] for j in range(0, terms.shape[1], 128)]
        )
        sums[i : i + 1, :] = jnp.sum(lanes.T, 0, keepdims=True)


def finish(own, kept, h2, h3, gain, head, weights, token, part, hidden):
    rows, width = kept.shape
    step, depth = h2.shape
    specs = [
        pl.BlockSpec(memory_space=pltpu.SMEM),
        pl.BlockSpec((step, width), lambda i: (part, 0)),
        pl.BlockSpec((step, depth), lambda i: (0, 0)),
        pl.BlockSpec((step, depth), lambda i: (0, 0)),
        pl.BlockSpec((1, width), lambda i: (0, 0)),
        pl.BlockSpec((1, width), lambda i: (0, 0)),
        *(pl.BlockSpec(w.shape, lambda i: (0, 0)) for w in weights),
    ]
    specs.append(far_memory())
    args = [own, kept, h2, h3, gain, head, *weights, token]
    aliases = {}
    if hidden is not None:
        aliases = {len(args): 0}
        specs.append(pl.BlockSpec(memory_space=pl.ANY))
        args.append(hidden)
    return pl.pallas_call(
        finish_kernel,
        grid=(1,),
        in_specs=specs,
        out_specs=(
            pl.BlockSpec((step, width), lambda i: (part, 0)),
            pl.BlockSpec((2, step), lambda i: (0, 0)),
        ),
        out_shape=(
            jax.ShapeDtypeStruct((rows, width), jnp.bfloat16),
            jax.ShapeDtypeStruct((2, step), jnp.float32),
        ),
        input_output_aliases=aliases,
        compiler_params=params(14),
        cost_estimate=cost(4 * step * depth * width, 8 * step * width),
        name="finish",
    )(*args)


def flip(x, bit):
    count = lax.axis_size("tensor")
    return lax.ppermute(x, "tensor", [(i, i ^ bit) for i in range(count)])


def swap_parts(x):
    return lax.ppermute(x, "parts", [(0, 1), (1, 0)])


def chunk_sizes(rows, n_dp):
    if n_dp > 8 or rows % 256:
        return (rows,)
    return (rows // 2, rows // 2)


def on_device(
    hidden_in,
    row_loads,
    seg_ids,
    pos_ids,
    prompt_order,
    attn_gain,
    w_query,
    key_matrix,
    value_matrix,
    w_out,
    final_gain,
    value_head,
):
    n_dp = lax.axis_size("dp")
    me = lax.axis_index("dp")
    t = lax.axis_index("tensor")
    rows, width = hidden_in.shape
    sizes = chunk_sizes(rows, n_dp)

    own = [hidden_in[sum(sizes[:c]) : sum(sizes[: c + 1])] for c in range(len(sizes))]
    across = [flip(x, 2) for x in own]
    pair = flip(hidden_in, 1)

    lines = rows // QUERY_BLOCK
    digits, cos, sin = prep(
        row_loads, seg_ids.reshape(lines, QUERY_BLOCK), pos_ids.reshape(lines, QUERY_BLOCK)
    )
    gain = attn_gain.reshape(1, -1)
    t_own = jnp.stack([t, lax.axis_index("parts"), me]).astype(jnp.int32)
    acc, squares, far_weights, token = early(
        t_own, hidden_in, pair, gain, w_query, key_matrix, value_matrix
    )

    near, send_near, far2, far3, token = columns(t_own, w_out, token, width)
    near_other = flip(send_near, 1)

    q_parts, kv_parts = [], [[] for _ in range(n_dp)]
    for c in range(len(sizes)):
        received, token = lax.optimization_barrier((across[c], token))
        if c == len(sizes) - 1:
            far2, far3, token = lax.optimization_barrier((far2, far3, token))
            far2, far3 = flip(far2, 2), flip(far3, 3)
        if c > 0:
            for d in range(1, n_dp):
                kv_parts[d][-1], token = lax.optimization_barrier((kv_parts[d][-1], token))
        received, token = lax.optimization_barrier((received, token))
        diagonal = flip(received, 1)
        if c > 0:
            near_other, token = lax.optimization_barrier((near_other, token))
        last = c == len(sizes) - 1
        soon = [(0, i) for i in range(c)] + [(d, i) for d in range(1, n_dp) for i in range(c)] if last else []
        q, kv, *side, token = late(
            sum(sizes[:c]),
            t_own,
            token,
            acc,
            squares,
            received,
            diagonal,
            gain,
            far_weights,
            cos,
            sin,
            digits,
            last,
            q_parts if last else [],
            [(d, sizes[i]) for d, i in soon],
            [kv_parts[d][i] for d, i in soon],
        )
        q_parts.append(q)
        kv_parts[0].append(kv)
        for d in range(1, n_dp):
            kv_parts[d].append(lax.ppermute(kv, "dp", [(i, (i + d) % n_dp) for i in range(n_dp)]))

    order = prompt_order.reshape(1, rows)
    q_all, (kv_all, keys) = q, side
    *state, token = attend(t_own, q_all, kv_all, keys)
    far3, token = lax.optimization_barrier((far3, token))
    other3 = swap_parts(far3)
    heads, *parts = attend_rest(
        t_own,
        q_all,
        state,
        keys,
        [(d, sizes[-1]) for d in range(1, n_dp)],
        [kv_parts[d][-1] for d in range(1, n_dp)],
        token,
        order,
    )
    heads2 = [flip(parts[0], 2)]
    rest, far2, other3 = lax.optimization_barrier((parts[1], far2, other3))
    heads2.append(flip(rest, 2))
    other2 = swap_parts(far2)
    weights = (far2, other2, far3, other3)
    heads_other = flip(heads, 1)
    kept, token = keep(order, hidden_in, heads, heads_other, near, near_other)
    heads2[0], token = lax.optimization_barrier((heads2[0], token))
    heads3 = [flip(x, 1) for x in heads2]
    final = final_gain.astype(jnp.float32).reshape(1, width)
    head = value_head.astype(jnp.float32).reshape(1, width)
    hidden, values = None, []
    for j in range(N_PART):
        hidden, sums = finish(
            t_own, kept, heads2[j], heads3[j], final, head, weights, token, j, hidden
        )
        square, product = sums + flip(sums, 1) + (flip(sums, 2) + flip(sums, 3))
        values.append(product * lax.rsqrt(square / MODEL_WIDTH + NORM_EPS))
    return hidden, jnp.concatenate(values)


def solution(mesh):
    return jax.shard_map(
        on_device,
        mesh=mesh,
        in_specs=(
            P(("parts", "dp"), "tensor"),
            P(("parts", "dp"), None),
            P(("parts", "dp")),
            P(("parts", "dp")),
            P(("parts", "dp"), None),
            P(),
            P(None, "tensor"),
            P(None, "tensor"),
            P(None, "tensor"),
            P("tensor", None),
            P("tensor"),
            P("tensor"),
        ),
        out_specs=(P(("parts", "dp"), "tensor"), P(("parts", "dp"))),
        check_vma=False,
    )
```

```python
import functools
import math

import jax
import jax.numpy as jnp
from jax import lax
from jax.experimental import pallas as pl
from jax.experimental.pallas import tpu as pltpu
from jax.sharding import PartitionSpec as P

MODEL_WIDTH = 4096
HEAD_WIDTH = 128
NORM_EPS = 1e-05
ROPE_BASE = 500000.0

SEG_SPAN = 64
POS_SPAN = 1024
POS_DIGIT = 128
DIGIT_ROWS = 16
N_PART = 2

QUERY_BLOCK = 128
KEY_BLOCK = 256
MASKED = -1e30

VMEM = pltpu.VMEM
EARLY_MIB = 16
TOKEN = jax.ShapeDtypeStruct((8, 128), jnp.float32)


def params(limit_mib):
    return pltpu.CompilerParams(vmem_limit_bytes=limit_mib * 2**20)


def cost(flops, bytes_accessed):
    return pl.CostEstimate(flops=flops, bytes_accessed=bytes_accessed, transcendentals=0)


def whole():
    return pl.BlockSpec(memory_space=VMEM)


def far_memory():
    return pl.BlockSpec(memory_space=pltpu.HBM)


def prep_kernel(loads, seg, pos, digits, cos, sin):
    lines, lanes = seg.shape
    row = lanes * lax.broadcasted_iota(jnp.int32, seg.shape, 0) + lax.broadcasted_iota(jnp.int32, seg.shape, 1)
    dest = jnp.zeros(seg.shape, jnp.int32)
    total = 0
    for e in range(loads.shape[1]):
        total = total + loads[0, e]
        dest += jnp.where(row >= total, 1, 0)
    low_pos = lax.bitwise_and(pos[...], POS_DIGIT - 1)
    high_pos = lax.shift_right_logical(pos[...], POS_DIGIT.bit_length() - 1)
    digits[...] = jnp.zeros(digits.shape, digits.dtype)
    for j, digit in enumerate((low_pos, high_pos, seg[...], dest)):
        line = jnp.concatenate([digit[i : i + 1, :] for i in range(lines)], 1)
        digits[j : j + 1, :] = line.astype(jnp.float32).astype(digits.dtype)
    at = pos[...].astype(jnp.float32)
    half = HEAD_WIDTH // 2
    lane = lax.broadcasted_iota(jnp.int32, (lanes, HEAD_WIDTH), 1)
    low = lane < half
    power = jnp.where(low, lane, lane - half).astype(jnp.float32)
    inverse = jnp.exp(power * (-2.0 * math.log(ROPE_BASE) / HEAD_WIDTH))
    for i in range(lines):
        column = jnp.broadcast_to(at[i : i + 1, :], (lanes, lanes)).T
        angle = column * inverse
        span = slice(i * lanes, (i + 1) * lanes)
        sine = jnp.sin(angle)
        cos[span, :] = jnp.cos(angle)
        sin[span, :] = jnp.where(low, -sine, sine)


def prep(row_loads, seg, pos):
    lines, lanes = seg.shape
    rows = lines * lanes
    table = jax.ShapeDtypeStruct((rows, HEAD_WIDTH), jnp.float32)
    return pl.pallas_call(
        prep_kernel,
        out_shape=(jax.ShapeDtypeStruct((DIGIT_ROWS, rows), jnp.bfloat16), table, table),
        in_specs=[pl.BlockSpec(memory_space=pltpu.SMEM), whole(), whole()],
        out_specs=(whole(), whole(), whole()),
        compiler_params=params(6),
        cost_estimate=cost(2 * 10**9, 4 * 10**7),
        name="prep",
    )(row_loads, seg, pos)


def gained(piece, gain, number):
    x = piece[...].astype(jnp.float32)
    width = x.shape[1]
    factor = gain[:, pl.ds(pl.multiple_of(number * width, width), width)].astype(jnp.float32)
    return jnp.sum(x * x, -1, keepdims=True), (x * factor).astype(jnp.bfloat16)


def weight_copies(weights, to, sem, ids, width):
    copies = []
    for i, number in enumerate(ids):
        at = 0
        rows = pl.ds(pl.multiple_of(number * width, width), width)
        for weight in weights:
            columns = pl.ds(at, weight.shape[1])
            copies.append(pltpu.make_async_copy(weight.at[rows, :], to.at[i, :, columns], sem.at[len(copies)]))
            at += weight.shape[1]
    return copies


def start(copies):
    for copy in copies:
        copy.start()


def wait(copies):
    for copy in copies:
        copy.wait()


def early_kernel(own, r0, r1, gain, wq, wk, wv, acc, squares, far_weights, token, held, sem):
    del token
    width = r0.shape[1]
    t = own[0]
    near = weight_copies((wq, wk, wv), held, sem.at[0], (t, lax.bitwise_xor(t, 1)), width)
    far = weight_copies(
        (wq, wk, wv), far_weights, sem.at[1], (lax.bitwise_xor(t, 2), lax.bitwise_xor(t, 3)), width
    )
    start(near)
    start(far)
    square0, x0 = gained(r0, gain, t)
    wait(near[:3])
    acc[...] = jnp.dot(x0, held[0], preferred_element_type=jnp.float32)
    square1, x1 = gained(r1, gain, lax.bitwise_xor(t, 1))
    wait(near[3:])
    acc[...] += jnp.dot(x1, held[1], preferred_element_type=jnp.float32)
    squares[...] = square0 + square1
    wait(far)


def early(own, r0, r1, gain, wq, wk, wv):
    rows, width = r0.shape
    columns = wq.shape[1] + wk.shape[1] + wv.shape[1]
    half = (2, width, columns)
    return pl.pallas_call(
        early_kernel,
        out_shape=(
            jax.ShapeDtypeStruct((rows, columns), jnp.float32),
            jax.ShapeDtypeStruct((rows, 1), jnp.float32),
            jax.ShapeDtypeStruct(half, jnp.bfloat16),
            TOKEN,
        ),
        in_specs=[pl.BlockSpec(memory_space=pltpu.SMEM)] + [whole()] * 3 + [far_memory()] * 3,
        out_specs=(whole(), whole(), whole(), far_memory()),
        scratch_shapes=[VMEM(half, jnp.bfloat16), pltpu.SemaphoreType.DMA((2, 6))],
        compiler_params=params(12),
        cost_estimate=cost(4 * rows * width * columns, 8 * width * columns),
        name="early",
    )(own, r0, r1, gain, wq, wk, wv)


def digit_lines(rows):
    return [(i, min(2 * HEAD_WIDTH, rows - i)) for i in range(0, rows, 2 * HEAD_WIDTH)]


def keys_of(digits, back, own):
    digit = digits.astype(jnp.float32).astype(jnp.int32)
    doc = digit[3:4] * SEG_SPAN + digit[2:3]
    key = doc * POS_SPAN + digit[1:2] * POS_DIGIT + digit[0:1]
    return jnp.where(back <= own[2], key, -1)


def unpack(pieces, sources, own, kv_all, keys):
    lanes = keys.shape[1]
    row = 0
    for (back, size), source in zip(pieces, sources, strict=True):
        kv_all[row : row + size, :] = source[:size, :]
        for i, (line, count) in enumerate(digit_lines(size)):
            at = size + i * DIGIT_ROWS
            key = keys_of(source[at : at + DIGIT_ROWS, :count], back, own)
            for j in range(0, count, lanes):
                to = (row + line + j) // lanes
                keys[to : to + 1, :] = key[:, j : j + lanes]
        row += size


def late_kernel(at, pieces, own, before, acc, squares, r2, r3, gain, weights, cos, sin, digits, *refs):
    del before
    refs = list(refs)
    rows = r2.shape[0]
    n_old = sum(1 for back, _ in pieces if back == 0)
    q_old, kv_old = refs[:n_old], refs[n_old : n_old + len(pieces)]
    q_out, kv_out, *outs = refs[n_old + len(pieces) :]
    span = slice(at, at + rows)
    square2, x2 = gained(r2, gain, lax.bitwise_xor(own[0], 2))
    total = acc[span, :] + jnp.dot(x2, weights[0], preferred_element_type=jnp.float32)
    square3, x3 = gained(r3, gain, lax.bitwise_xor(own[0], 3))
    total += jnp.dot(x3, weights[1], preferred_element_type=jnp.float32)
    total *= lax.rsqrt((squares[span, :] + square2 + square3) / MODEL_WIDTH + NORM_EPS)
    cosine, sine = cos[span, :], sin[span, :]
    n_head = q_out.shape[0]

    def rope(x):
        return (x * cosine + pltpu.roll(x, HEAD_WIDTH // 2, 1) * sine).astype(jnp.bfloat16)

    here = slice(at, at + rows) if q_out.shape[1] > rows else slice(0, rows)
    for h in range(n_head):
        q_out[h, here, :] = rope(total[:, h * HEAD_WIDTH : (h + 1) * HEAD_WIDTH])
    kv_out[:rows, :HEAD_WIDTH] = rope(total[:, n_head * HEAD_WIDTH : (n_head + 1) * HEAD_WIDTH])
    kv_out[:rows, HEAD_WIDTH:] = total[:, (n_head + 1) * HEAD_WIDTH :].astype(jnp.bfloat16)
    for i, (line, count) in enumerate(digit_lines(rows)):
        to = rows + i * DIGIT_ROWS
        kv_out[to : to + DIGIT_ROWS, :count] = digits[:, at + line : at + line + count]
    if len(outs) > 1:
        kv_all, keys, _ = outs
        row = 0
        for q in q_old:
            q_out[:, row : row + q.shape[1], :] = q[...]
            row += q.shape[1]
        sources = [*kv_old[:n_old], kv_out, *kv_old[n_old:]]
        unpack([*pieces[:n_old], (0, rows), *pieces[n_old:]], sources, own, kv_all, keys)


def late(at, own, before, acc, squares, r2, r3, gain, weights, cos, sin, digits, last, q_old, pieces, kv_old):
    rows, width = r2.shape
    columns = acc.shape[1]
    heads = columns // HEAD_WIDTH - 2
    n_key = rows + sum(size for _, size in pieces)
    more, specs = (), ()
    if last:
        more = (
            jax.ShapeDtypeStruct((n_key, 2 * HEAD_WIDTH), jnp.bfloat16),
            jax.ShapeDtypeStruct((n_key // QUERY_BLOCK, QUERY_BLOCK), jnp.int32),
        )
        specs = (whole(), whole())
    return pl.pallas_call(
        functools.partial(late_kernel, at, tuple(pieces)),
        out_shape=(
            jax.ShapeDtypeStruct((heads, at + rows if last else rows, HEAD_WIDTH), jnp.bfloat16),
            jax.ShapeDtypeStruct((rows + DIGIT_ROWS * len(digit_lines(rows)), 2 * HEAD_WIDTH), jnp.bfloat16),
            *more,
            TOKEN,
        ),
        in_specs=[pl.BlockSpec(memory_space=pltpu.SMEM), far_memory()]
        + [whole()] * (9 + len(q_old) + len(kv_old)),
        out_specs=(whole(), whole(), *specs, far_memory()),
        compiler_params=params(10),
        cost_estimate=cost(4 * rows * width * columns, 4 * width * columns),
        name="late",
    )(own, before, acc, squares, r2, r3, gain, weights, cos, sin, digits, *q_old, *kv_old)


def pick_rows(order, x):
    rows = x.shape[0]
    pick = (order == lax.broadcasted_iota(jnp.int32, (rows, rows), 0)).astype(jnp.bfloat16)
    return lax.dot_general(pick, x, (((0,), (0,)), ((), ())), preferred_element_type=jnp.float32)


def attend_kernel(pieces, last, own, q_all, *refs):
    refs = list(refs)

    def take(count):
        taken = refs[:count]
        del refs[:count]
        return taken

    n_head, rows, _ = q_all.shape
    n_query = rows // QUERY_BLOCK
    if last:
        m_in, l_in, acc_in, own_keys = take(4)
        kv_in = take(len(pieces))
        _, order, out, *parts = take(3 + N_PART)
        heads, kv_all, keys = take(3)
        unpack(pieces, kv_in, own, kv_all, keys)
        own_line = kv_all.shape[0] // QUERY_BLOCK
        keys[own_line : own_line + n_query, :] = own_keys[:n_query, :]
    else:
        kv_all, keys, m_out, l_out, acc_out, _ = take(6)
        own_line = 0
    m_s, l_s, acc_s, keys_s, sem = refs
    n_key = kv_all.shape[0] // KEY_BLOCK
    lanes = keys.shape[1]
    copy = pltpu.make_async_copy(keys, keys_s, sem)
    copy.start()
    copy.wait()
    scale = 1.4426950408889634 / HEAD_WIDTH**0.5
    stacked = n_head * QUERY_BLOCK
    lines = KEY_BLOCK // lanes

    def block(qb, _):
        at = pl.ds(pl.multiple_of(qb * QUERY_BLOCK, QUERY_BLOCK), QUERY_BLOCK)
        flat = pl.ds(pl.multiple_of(qb * stacked, stacked), stacked)
        q = q_all[:, at, :].reshape(stacked, HEAD_WIDTH)
        high = jnp.broadcast_to(keys[pl.ds(own_line + qb, 1), :], (QUERY_BLOCK, lanes)).T
        low = high - lax.bitwise_and(high, POS_SPAN - 1)
        high, low = (jnp.concatenate([x] * lines, 1) for x in (high, low))
        lowest = keys_s[own_line + qb, 0]
        lowest = lowest - lax.bitwise_and(lowest, POS_SPAN - 1)
        highest = lax.bitwise_or(keys_s[own_line + qb, lanes - 1], POS_SPAN - 1)
        if not last:
            m_s[...] = jnp.full(m_s.shape, MASKED, jnp.float32)
            l_s[...] = jnp.zeros(l_s.shape, jnp.float32)
            acc_s[...] = jnp.zeros(acc_s.shape, jnp.float32)
        else:
            m_s[...] = m_in[flat, :]
            l_s[...] = l_in[flat, :]
            acc_s[...] = acc_in[flat, :]

        def some_keys(index, _):
            @pl.when((keys_s[index * lines + lines - 1, lanes - 1] >= lowest) & (keys_s[index * lines, 0] <= highest))
            def _():
                span = pl.ds(pl.multiple_of(index * KEY_BLOCK, KEY_BLOCK), KEY_BLOCK)
                k = kv_all[span, :HEAD_WIDTH]
                v = kv_all[span, HEAD_WIDTH:]
                s = lax.dot_general(q, k, (((1,), (1,)), ((), ())), preferred_element_type=jnp.float32)
                ids = jnp.concatenate([keys[pl.ds(index * lines + i, 1), :] for i in range(lines)], 1)
                allowed = (ids <= high) & (ids >= low)
                s = jnp.where(allowed[None], (s * scale).reshape(n_head, QUERY_BLOCK, KEY_BLOCK), MASKED)
                s = s.reshape(stacked, KEY_BLOCK)
                m_old = m_s[...]
                m_new = jnp.maximum(m_old, jnp.max(s, -1, keepdims=True))
                alpha = jnp.exp2(m_old - m_new)
                p = [
                    jnp.exp2(s[:, i : i + HEAD_WIDTH] - m_new) for i in range(0, KEY_BLOCK, HEAD_WIDTH)
                ]
                m_s[...] = m_new
                l_s[...] = l_s[...] * alpha + functools.reduce(jnp.add, p)
                p = jnp.concatenate(p, 1).astype(jnp.bfloat16)
                acc_s[...] = acc_s[...] * alpha + jnp.dot(p, v, preferred_element_type=jnp.float32)

            return 0

        lax.fori_loop(0, n_key, some_keys, 0)
        if last:
            done = (acc_s[...] / jnp.sum(l_s[...], -1, keepdims=True)).astype(jnp.bfloat16)
            for h in range(n_head):
                heads[at, h * HEAD_WIDTH : (h + 1) * HEAD_WIDTH] = done[h * QUERY_BLOCK : (h + 1) * QUERY_BLOCK]
        else:
            m_out[flat, :] = m_s[...]
            l_out[flat, :] = l_s[...]
            acc_out[flat, :] = acc_s[...]
        return 0

    lax.fori_loop(0, n_query, block, 0)
    if last:
        picked = pick_rows(order[...], heads[...]).astype(jnp.bfloat16)
        out[...] = picked
        for i, part in enumerate(parts):
            part[...] = picked[i * part.shape[0] : (i + 1) * part.shape[0], :]


def attend(own, q_all, kv_all, keys):
    n_head, rows, _ = q_all.shape
    stacked = n_head * QUERY_BLOCK
    n_key = kv_all.shape[0]
    running = jax.ShapeDtypeStruct((n_head * rows, HEAD_WIDTH), jnp.float32)
    return pl.pallas_call(
        functools.partial(attend_kernel, (), False),
        out_shape=(running,) * 3 + (TOKEN,),
        in_specs=[pl.BlockSpec(memory_space=pltpu.SMEM)] + [whole()] * 3,
        out_specs=(whole(),) * 3 + (far_memory(),),
        scratch_shapes=[VMEM((stacked, HEAD_WIDTH), jnp.float32)] * 3
        + [pltpu.SMEM(keys.shape, jnp.int32), pltpu.SemaphoreType.DMA(())],
        compiler_params=params(12),
        cost_estimate=cost(4 * rows * n_key * n_head * HEAD_WIDTH, 4 * rows * n_head * HEAD_WIDTH),
        name="attend",
    )(own, q_all, kv_all, keys)


def attend_rest(own, q_all, state, own_keys, pieces, kv_parts, token, order):
    n_head, rows, _ = q_all.shape
    stacked = n_head * QUERY_BLOCK
    n_key = sum(size for _, size in pieces)
    key_lines = ((n_key + rows) // QUERY_BLOCK, QUERY_BLOCK)
    return pl.pallas_call(
        functools.partial(attend_kernel, tuple(pieces), True),
        out_shape=tuple(
            jax.ShapeDtypeStruct((size, n_head * HEAD_WIDTH), jnp.bfloat16)
            for size in [rows] + [rows // N_PART] * N_PART
        ),
        in_specs=[pl.BlockSpec(memory_space=pltpu.SMEM)]
        + [whole()] * (5 + len(pieces))
        + [far_memory(), whole()],
        out_specs=(whole(),) * (1 + N_PART),
        scratch_shapes=[
            VMEM((rows, n_head * HEAD_WIDTH), jnp.bfloat16),
            VMEM((n_key, 2 * HEAD_WIDTH), jnp.bfloat16),
            VMEM(key_lines, jnp.int32),
        ]
        + [VMEM((stacked, HEAD_WIDTH), jnp.float32)] * 3
        + [pltpu.SMEM(key_lines, jnp.int32), pltpu.SemaphoreType.DMA(())],
        compiler_params=params(12 + n_key // 512),
        cost_estimate=cost(4 * rows * n_key * n_head * HEAD_WIDTH, 4 * rows * n_head * HEAD_WIDTH),
        name="attend_rest",
    )(own, q_all, *state, own_keys, *kv_parts, token, order)


def columns_kernel(own, w_out, token_in, near, send_near, far, beside, token, sem):
    del token_in, token
    depth, width = near.shape
    half = depth // 2
    copies = []
    for bits, first, to in (
        (2, own[1] * half, far),
        (3, own[1] * half, beside),
        (1, 0, send_near),
        (0, 0, near),
    ):
        rows = pl.ds(pl.multiple_of(first, half), to.shape[0])
        at = pl.ds(pl.multiple_of(lax.bitwise_xor(own[0], bits) * width, width), width)
        copies.append(pltpu.make_async_copy(w_out.at[rows, at], to, sem.at[len(copies)]))
    start(copies)
    wait(copies)


def columns(own, w_out, token, width):
    rows = w_out.shape[0]
    blocks = [jax.ShapeDtypeStruct((size, width), w_out.dtype) for size in (rows, rows, rows // 2, rows // 2)]
    return pl.pallas_call(
        columns_kernel,
        out_shape=(*blocks, TOKEN),
        in_specs=[pl.BlockSpec(memory_space=pltpu.SMEM), far_memory(), far_memory()],
        out_specs=(whole(),) * 4 + (far_memory(),),
        scratch_shapes=[pltpu.SemaphoreType.DMA((5,))],
        compiler_params=params(6),
        cost_estimate=cost(1, 4 * w_out.size),
        name="columns",
    )(own, w_out, token)


def keep_kernel(order, own, h0, h1, w0, w1, out, token):
    del token
    total = jnp.dot(h0[...], w0[...], preferred_element_type=jnp.float32)
    total += jnp.dot(h1[...], w1[...], preferred_element_type=jnp.float32)
    out[...] = total + pick_rows(order[...], own[...])


def keep(order, own, h0, h1, w0, w1):
    rows, width = own.shape
    depth = h0.shape[1]
    return pl.pallas_call(
        keep_kernel,
        out_shape=(jax.ShapeDtypeStruct((rows, width), jnp.float32), TOKEN),
        in_specs=[whole()] * 6,
        out_specs=(whole(), far_memory()),
        compiler_params=params(12),
        cost_estimate=cost(2 * rows * (2 * depth + rows) * width, 4 * depth * width + 6 * rows * width),
        name="keep",
    )(order, own, h0, h1, w0, w1)


def shares(own, h):
    half = h.shape[1] // 2
    return tuple(pl.ds(pl.multiple_of(share * half, half), half) for share in (own[1], 1 - own[1]))


def gather_kernel(own, kept, *refs):
    *heads, w2, w3, other3, out = refs
    rows = heads[0].shape[0]
    for j in range(N_PART):
        span = slice(j * rows, (j + 1) * rows)
        h2, h3 = heads[j], heads[N_PART + j]
        mine, others = shares(own, h2)
        total = kept[span, :]
        for h, columns, weight in ((h2, mine, w2), (h3, mine, w3), (h3, others, other3)):
            total += jnp.dot(h[:, columns], weight[...], preferred_element_type=jnp.float32)
        out[span, :] = total


def gather(own, kept, heads2, heads3, w2, w3, other3):
    rows, width = kept.shape
    depth = heads2[0].shape[1]
    return pl.pallas_call(
        gather_kernel,
        out_shape=jax.ShapeDtypeStruct((rows, width), jnp.float32),
        in_specs=[pl.BlockSpec(memory_space=pltpu.SMEM)] + [whole()] * (4 + 2 * N_PART),
        out_specs=whole(),
        compiler_params=params(14),
        cost_estimate=cost(3 * rows * depth * width, 8 * rows * width),
        name="gather",
    )(own, kept, *heads2, *heads3, w2, w3, other3)


def finish_kernel(own, most, *refs):
    *heads, other2, gain, head, hidden_out, sums = refs
    rows = heads[0].shape[0]
    weight = gain[...].astype(jnp.float32) * head[...].astype(jnp.float32)
    for j, h in enumerate(heads):
        span = slice(j * rows, (j + 1) * rows)
        _, others = shares(own, h)
        total = most[span, :] + jnp.dot(h[:, others], other2[...], preferred_element_type=jnp.float32)
        hidden = total.astype(jnp.bfloat16)
        hidden_out[span, :] = hidden
        x = hidden.astype(jnp.float32)
        for i, terms in enumerate((x * x, x * weight)):
            lanes = functools.reduce(jnp.add, [terms[:, k : k + 128] for k in range(0, terms.shape[1], 128)])
            sums[i : i + 1, span] = jnp.sum(lanes.T, 0, keepdims=True)


def finish(own, most, heads2, other2, gain, head):
    rows, width = most.shape
    depth = heads2[0].shape[1]
    return pl.pallas_call(
        finish_kernel,
        out_shape=(
            jax.ShapeDtypeStruct((rows, width), jnp.bfloat16),
            jax.ShapeDtypeStruct((2, rows), jnp.float32),
        ),
        in_specs=[pl.BlockSpec(memory_space=pltpu.SMEM)] + [whole()] * (4 + N_PART),
        out_specs=(whole(), whole()),
        compiler_params=params(14),
        cost_estimate=cost(rows * depth * width, 8 * rows * width),
        name="finish",
    )(own, most, *heads2, other2, gain, head)


def flip(x, bit):
    count = lax.axis_size("tensor")
    return lax.ppermute(x, "tensor", [(i, i ^ bit) for i in range(count)])


def swap_parts(x):
    return lax.ppermute(x, "parts", [(0, 1), (1, 0)])


def chunk_sizes(rows, n_dp):
    if n_dp > 8 or rows % 256:
        return (rows,)
    return (rows // 2, rows // 2)


def on_device(
    hidden_in,
    row_loads,
    seg_ids,
    pos_ids,
    prompt_order,
    attn_gain,
    w_query,
    key_matrix,
    value_matrix,
    w_out,
    final_gain,
    value_head,
):
    n_dp = lax.axis_size("dp")
    me = lax.axis_index("dp")
    t = lax.axis_index("tensor")
    rows, width = hidden_in.shape
    sizes = chunk_sizes(rows, n_dp)

    own = [hidden_in[sum(sizes[:c]) : sum(sizes[: c + 1])] for c in range(len(sizes))]
    across = [flip(x, 2) for x in own]
    pair = flip(hidden_in, 1)

    lines = rows // QUERY_BLOCK
    digits, cos, sin = prep(
        row_loads, seg_ids.reshape(lines, QUERY_BLOCK), pos_ids.reshape(lines, QUERY_BLOCK)
    )
    gain = attn_gain.reshape(1, -1)
    t_own = jnp.stack([t, lax.axis_index("parts"), me]).astype(jnp.int32)
    acc, squares, far_weights, token = early(
        t_own, hidden_in, pair, gain, w_query, key_matrix, value_matrix
    )

    near, send_near, far2, far3, token = columns(t_own, w_out, token, width)
    near_other = flip(send_near, 1)

    q_parts, kv_parts = [], [[] for _ in range(n_dp)]
    for c in range(len(sizes)):
        received, token = lax.optimization_barrier((across[c], token))
        if c == len(sizes) - 1:
            far2, far3, token = lax.optimization_barrier((far2, far3, token))
            far2, far3 = flip(far2, 2), flip(far3, 3)
        if c > 0:
            for d in range(1, n_dp):
                kv_parts[d][-1], token = lax.optimization_barrier((kv_parts[d][-1], token))
        received, token = lax.optimization_barrier((received, token))
        diagonal = flip(received, 1)
        if c > 0:
            near_other, token = lax.optimization_barrier((near_other, token))
        last = c == len(sizes) - 1
        soon = [(0, i) for i in range(c)] + [(d, i) for d in range(1, n_dp) for i in range(c)] if last else []
        q, kv, *side, token = late(
            sum(sizes[:c]),
            t_own,
            token,
            acc,
            squares,
            received,
            diagonal,
            gain,
            far_weights,
            cos,
            sin,
            digits,
            last,
            q_parts if last else [],
            [(d, sizes[i]) for d, i in soon],
            [kv_parts[d][i] for d, i in soon],
        )
        q_parts.append(q)
        kv_parts[0].append(kv)
        for d in range(1, n_dp):
            kv_parts[d].append(lax.ppermute(kv, "dp", [(i, (i + d) % n_dp) for i in range(n_dp)]))

    order = prompt_order.reshape(1, rows)
    q_all, (kv_all, keys) = q, side
    *state, token = attend(t_own, q_all, kv_all, keys)
    far3, token = lax.optimization_barrier((far3, token))
    other3 = swap_parts(far3)
    heads, *parts = attend_rest(
        t_own,
        q_all,
        state,
        keys,
        [(d, sizes[-1]) for d in range(1, n_dp)],
        [kv_parts[d][-1] for d in range(1, n_dp)],
        token,
        order,
    )
    heads2 = [flip(parts[0], 2)]
    rest, far2 = lax.optimization_barrier((parts[1], far2))
    heads2.append(flip(rest, 2))
    other2 = swap_parts(far2)
    heads_other = flip(heads, 1)
    heads_other, other3 = lax.optimization_barrier((heads_other, other3))
    kept, token = keep(order, hidden_in, heads, heads_other, near, near_other)
    heads2[0], token = lax.optimization_barrier((heads2[0], token))
    heads3 = [flip(x, 1) for x in heads2]
    most = gather(t_own, kept, heads2, heads3, far2, far3, other3)
    hidden, sums = finish(
        t_own, most, heads2, other2, final_gain.reshape(1, width), value_head.reshape(1, width)
    )
    square, product = sums + flip(sums, 1) + (flip(sums, 2) + flip(sums, 3))
    return hidden, product * lax.rsqrt(square / MODEL_WIDTH + NORM_EPS)


def solution(mesh):
    return jax.shard_map(
        on_device,
        mesh=mesh,
        in_specs=(
            P(("parts", "dp"), "tensor"),
            P(("parts", "dp"), None),
            P(("parts", "dp")),
            P(("parts", "dp")),
            P(("parts", "dp"), None),
            P(),
            P(None, "tensor"),
            P(None, "tensor"),
            P(None, "tensor"),
            P("tensor", None),
            P("tensor"),
            P("tensor"),
        ),
        out_specs=(P(("parts", "dp"), "tensor"), P(("parts", "dp"))),
        check_vma=False,
    )
```

```python
import functools
import math

import jax
import jax.numpy as jnp
from jax import lax
from jax.experimental import pallas as pl
from jax.experimental.pallas import tpu as pltpu
from jax.sharding import PartitionSpec as P

MODEL_WIDTH = 4096
HEAD_WIDTH = 128
NORM_EPS = 1e-05
ROPE_BASE = 500000.0

SEG_SPAN = 64
POS_SPAN = 1024
POS_DIGIT = 128
DIGIT_ROWS = 16

QUERY_BLOCK = 128
KEY_BLOCK = 256
MASKED = -1e30

VMEM = pltpu.VMEM
EARLY_MIB = 16
TOKEN = jax.ShapeDtypeStruct((8, 128), jnp.float32)


def params(limit_mib):
    return pltpu.CompilerParams(vmem_limit_bytes=limit_mib * 2**20)


def cost(flops, bytes_accessed):
    return pl.CostEstimate(flops=flops, bytes_accessed=bytes_accessed, transcendentals=0)


def whole():
    return pl.BlockSpec(memory_space=VMEM)


def far_memory():
    return pl.BlockSpec(memory_space=pltpu.HBM)


def prep_kernel(loads, seg, pos, digits, cos, sin):
    lines, lanes = seg.shape
    row = lanes * lax.broadcasted_iota(jnp.int32, seg.shape, 0) + lax.broadcasted_iota(jnp.int32, seg.shape, 1)
    dest = jnp.zeros(seg.shape, jnp.int32)
    total = 0
    for e in range(loads.shape[1]):
        total = total + loads[0, e]
        dest += jnp.where(row >= total, 1, 0)
    low_pos = lax.bitwise_and(pos[...], POS_DIGIT - 1)
    high_pos = lax.shift_right_logical(pos[...], POS_DIGIT.bit_length() - 1)
    digits[...] = jnp.zeros(digits.shape, digits.dtype)
    for j, digit in enumerate((low_pos, high_pos, seg[...], dest)):
        line = jnp.concatenate([digit[i : i + 1, :] for i in range(lines)], 1)
        digits[j : j + 1, :] = line.astype(jnp.float32).astype(digits.dtype)
    at = pos[...].astype(jnp.float32)
    half = HEAD_WIDTH // 2
    lane = lax.broadcasted_iota(jnp.int32, (lanes, HEAD_WIDTH), 1)
    low = lane < half
    power = jnp.where(low, lane, lane - half).astype(jnp.float32)
    inverse = jnp.exp(power * (-2.0 * math.log(ROPE_BASE) / HEAD_WIDTH))
    for i in range(lines):
        column = jnp.broadcast_to(at[i : i + 1, :], (lanes, lanes)).T
        angle = column * inverse
        span = slice(i * lanes, (i + 1) * lanes)
        sine = jnp.sin(angle)
        cos[span, :] = jnp.cos(angle)
        sin[span, :] = jnp.where(low, -sine, sine)


def prep(row_loads, seg, pos):
    lines, lanes = seg.shape
    rows = lines * lanes
    table = jax.ShapeDtypeStruct((rows, HEAD_WIDTH), jnp.float32)
    return pl.pallas_call(
        prep_kernel,
        out_shape=(jax.ShapeDtypeStruct((DIGIT_ROWS, rows), jnp.bfloat16), table, table),
        in_specs=[pl.BlockSpec(memory_space=pltpu.SMEM), whole(), whole()],
        out_specs=(whole(), whole(), whole()),
        compiler_params=params(6),
        cost_estimate=cost(2 * 10**9, 4 * 10**7),
        name="prep",
    )(row_loads, seg, pos)


def gained(piece, gain, number):
    x = piece[...].astype(jnp.float32)
    width = x.shape[1]
    factor = gain[:, pl.ds(pl.multiple_of(number * width, width), width)].astype(jnp.float32)
    return jnp.sum(x * x, -1, keepdims=True), (x * factor).astype(jnp.bfloat16)


def weight_copies(weights, to, sem, ids, width):
    copies = []
    for i, number in enumerate(ids):
        at = 0
        rows = pl.ds(pl.multiple_of(number * width, width), width)
        for weight in weights:
            columns = pl.ds(at, weight.shape[1])
            copies.append(pltpu.make_async_copy(weight.at[rows, :], to.at[i, :, columns], sem.at[len(copies)]))
            at += weight.shape[1]
    return copies


def start(copies):
    for copy in copies:
        copy.start()


def wait(copies):
    for copy in copies:
        copy.wait()


def early_kernel(own, r0, r1, gain, wq, wk, wv, acc, squares, far_weights, token, held, sem):
    del token
    width = r0.shape[1]
    t = own[0]
    near = weight_copies((wq, wk, wv), held, sem.at[0], (t, lax.bitwise_xor(t, 1)), width)
    far = weight_copies(
        (wq, wk, wv), far_weights, sem.at[1], (lax.bitwise_xor(t, 2), lax.bitwise_xor(t, 3)), width
    )
    start(near)
    start(far)
    square0, x0 = gained(r0, gain, t)
    wait(near[:3])
    acc[...] = jnp.dot(x0, held[0], preferred_element_type=jnp.float32)
    square1, x1 = gained(r1, gain, lax.bitwise_xor(t, 1))
    wait(near[3:])
    acc[...] += jnp.dot(x1, held[1], preferred_element_type=jnp.float32)
    squares[...] = square0 + square1
    wait(far)


def early(own, r0, r1, gain, wq, wk, wv):
    rows, width = r0.shape
    columns = wq.shape[1] + wk.shape[1] + wv.shape[1]
    half = (2, width, columns)
    return pl.pallas_call(
        early_kernel,
        out_shape=(
            jax.ShapeDtypeStruct((rows, columns), jnp.float32),
            jax.ShapeDtypeStruct((rows, 1), jnp.float32),
            jax.ShapeDtypeStruct(half, jnp.bfloat16),
            TOKEN,
        ),
        in_specs=[pl.BlockSpec(memory_space=pltpu.SMEM)] + [whole()] * 3 + [far_memory()] * 3,
        out_specs=(whole(), whole(), whole(), far_memory()),
        scratch_shapes=[VMEM(half, jnp.bfloat16), pltpu.SemaphoreType.DMA((2, 6))],
        compiler_params=params(12),
        cost_estimate=cost(4 * rows * width * columns, 8 * width * columns),
        name="early",
    )(own, r0, r1, gain, wq, wk, wv)


def digit_lines(rows):
    return [(i, min(2 * HEAD_WIDTH, rows - i)) for i in range(0, rows, 2 * HEAD_WIDTH)]


def keys_of(digits, back, own):
    digit = digits.astype(jnp.float32).astype(jnp.int32)
    doc = digit[3:4] * SEG_SPAN + digit[2:3]
    key = doc * POS_SPAN + digit[1:2] * POS_DIGIT + digit[0:1]
    return jnp.where(back <= own[2], key, -1)


def unpack(pieces, sources, own, kv_all, keys):
    lanes = keys.shape[1]
    row = 0
    for (back, size), source in zip(pieces, sources, strict=True):
        kv_all[row : row + size, :] = source[:size, :]
        for i, (line, count) in enumerate(digit_lines(size)):
            at = size + i * DIGIT_ROWS
            key = keys_of(source[at : at + DIGIT_ROWS, :count], back, own)
            for j in range(0, count, lanes):
                to = (row + line + j) // lanes
                keys[to : to + 1, :] = key[:, j : j + lanes]
        row += size


def late_kernel(at, pieces, own, before, acc, squares, r2, r3, gain, weights, cos, sin, digits, *refs):
    del before
    refs = list(refs)
    rows = r2.shape[0]
    n_old = sum(1 for back, _ in pieces if back == 0)
    q_old, kv_old = refs[:n_old], refs[n_old : n_old + len(pieces)]
    q_out, kv_out, *outs = refs[n_old + len(pieces) :]
    span = slice(at, at + rows)
    square2, x2 = gained(r2, gain, lax.bitwise_xor(own[0], 2))
    total = acc[span, :] + jnp.dot(x2, weights[0], preferred_element_type=jnp.float32)
    square3, x3 = gained(r3, gain, lax.bitwise_xor(own[0], 3))
    total += jnp.dot(x3, weights[1], preferred_element_type=jnp.float32)
    total *= lax.rsqrt((squares[span, :] + square2 + square3) / MODEL_WIDTH + NORM_EPS)
    cosine, sine = cos[span, :], sin[span, :]
    n_head = q_out.shape[0]

    def rope(x):
        return (x * cosine + pltpu.roll(x, HEAD_WIDTH // 2, 1) * sine).astype(jnp.bfloat16)

    here = slice(at, at + rows) if q_out.shape[1] > rows else slice(0, rows)
    for h in range(n_head):
        q_out[h, here, :] = rope(total[:, h * HEAD_WIDTH : (h + 1) * HEAD_WIDTH])
    kv_out[:rows, :HEAD_WIDTH] = rope(total[:, n_head * HEAD_WIDTH : (n_head + 1) * HEAD_WIDTH])
    kv_out[:rows, HEAD_WIDTH:] = total[:, (n_head + 1) * HEAD_WIDTH :].astype(jnp.bfloat16)
    for i, (line, count) in enumerate(digit_lines(rows)):
        to = rows + i * DIGIT_ROWS
        kv_out[to : to + DIGIT_ROWS, :count] = digits[:, at + line : at + line + count]
    if len(outs) > 1:
        kv_all, keys, _ = outs
        row = 0
        for q in q_old:
            q_out[:, row : row + q.shape[1], :] = q[...]
            row += q.shape[1]
        sources = [*kv_old[:n_old], kv_out, *kv_old[n_old:]]
        unpack([*pieces[:n_old], (0, rows), *pieces[n_old:]], sources, own, kv_all, keys)


def late(at, own, before, acc, squares, r2, r3, gain, weights, cos, sin, digits, last, q_old, pieces, kv_old):
    rows, width = r2.shape
    columns = acc.shape[1]
    heads = columns // HEAD_WIDTH - 2
    n_key = rows + sum(size for _, size in pieces)
    more, specs = (), ()
    if last:
        more = (
            jax.ShapeDtypeStruct((n_key, 2 * HEAD_WIDTH), jnp.bfloat16),
            jax.ShapeDtypeStruct((n_key // QUERY_BLOCK, QUERY_BLOCK), jnp.int32),
        )
        specs = (whole(), whole())
    return pl.pallas_call(
        functools.partial(late_kernel, at, tuple(pieces)),
        out_shape=(
            jax.ShapeDtypeStruct((heads, at + rows if last else rows, HEAD_WIDTH), jnp.bfloat16),
            jax.ShapeDtypeStruct((rows + DIGIT_ROWS * len(digit_lines(rows)), 2 * HEAD_WIDTH), jnp.bfloat16),
            *more,
            TOKEN,
        ),
        in_specs=[pl.BlockSpec(memory_space=pltpu.SMEM), far_memory()]
        + [whole()] * (9 + len(q_old) + len(kv_old)),
        out_specs=(whole(), whole(), *specs, far_memory()),
        compiler_params=params(10),
        cost_estimate=cost(4 * rows * width * columns, 4 * width * columns),
        name="late",
    )(own, before, acc, squares, r2, r3, gain, weights, cos, sin, digits, *q_old, *kv_old)


def part_sizes(rows):
    return (rows // 2, rows // 2)


def pick_matrix(order, out):
    rows = out.shape[0]
    size = QUERY_BLOCK
    for i in range(0, rows, size):
        wanted = jnp.broadcast_to(order[:, i : i + size], (size, size)).T
        for j in range(0, rows, size):
            at = lax.broadcasted_iota(jnp.int32, (size, size), 1) + j
            out[i : i + size, j : j + size] = jnp.where(wanted == at, 1.0, 0.0).astype(out.dtype)


def pick_rows(pick, x):
    return jnp.dot(pick, x, preferred_element_type=jnp.float32)


def attend_kernel(pieces, last, own, q_all, *refs):
    refs = list(refs)

    def take(count):
        taken = refs[:count]
        del refs[:count]
        return taken

    n_head, rows, _ = q_all.shape
    n_query = rows // QUERY_BLOCK
    if last:
        m_in, l_in, acc_in, own_keys = take(4)
        kv_in = take(len(pieces))
        _, pick, out, *parts = take(5)
        heads, kv_all, keys = take(3)
        unpack(pieces, kv_in, own, kv_all, keys)
        own_line = kv_all.shape[0] // QUERY_BLOCK
        keys[own_line : own_line + n_query, :] = own_keys[:n_query, :]
    else:
        kv_all, keys, order, m_out, l_out, acc_out, pick, _ = take(8)
        own_line = 0
    m_s, l_s, acc_s, keys_s, sem = refs
    n_key = kv_all.shape[0] // KEY_BLOCK
    lanes = keys.shape[1]
    copy = pltpu.make_async_copy(keys, keys_s, sem)
    copy.start()
    copy.wait()
    scale = 1.4426950408889634 / HEAD_WIDTH**0.5
    stacked = n_head * QUERY_BLOCK
    lines = KEY_BLOCK // lanes

    def block(qb, _):
        at = pl.ds(pl.multiple_of(qb * QUERY_BLOCK, QUERY_BLOCK), QUERY_BLOCK)
        flat = pl.ds(pl.multiple_of(qb * stacked, stacked), stacked)
        q = q_all[:, at, :].reshape(stacked, HEAD_WIDTH)
        high = jnp.broadcast_to(keys[pl.ds(own_line + qb, 1), :], (QUERY_BLOCK, lanes)).T
        low = high - lax.bitwise_and(high, POS_SPAN - 1)
        high, low = (jnp.concatenate([x] * lines, 1) for x in (high, low))
        lowest = keys_s[own_line + qb, 0]
        lowest = lowest - lax.bitwise_and(lowest, POS_SPAN - 1)
        highest = lax.bitwise_or(keys_s[own_line + qb, lanes - 1], POS_SPAN - 1)
        if not last:
            m_s[...] = jnp.full(m_s.shape, MASKED, jnp.float32)
            l_s[...] = jnp.zeros(l_s.shape, jnp.float32)
            acc_s[...] = jnp.zeros(acc_s.shape, jnp.float32)
        else:
            m_s[...] = m_in[flat, :]
            l_s[...] = l_in[flat, :]
            acc_s[...] = acc_in[flat, :]

        def some_keys(index, _):
            @pl.when((keys_s[index * lines + lines - 1, lanes - 1] >= lowest) & (keys_s[index * lines, 0] <= highest))
            def _():
                span = pl.ds(pl.multiple_of(index * KEY_BLOCK, KEY_BLOCK), KEY_BLOCK)
                k = kv_all[span, :HEAD_WIDTH]
                v = kv_all[span, HEAD_WIDTH:]
                s = lax.dot_general(q, k, (((1,), (1,)), ((), ())), preferred_element_type=jnp.float32)
                ids = jnp.concatenate([keys[pl.ds(index * lines + i, 1), :] for i in range(lines)], 1)
                allowed = (ids <= high) & (ids >= low)
                s = jnp.where(allowed[None], (s * scale).reshape(n_head, QUERY_BLOCK, KEY_BLOCK), MASKED)
                s = s.reshape(stacked, KEY_BLOCK)
                m_old = m_s[...]
                m_new = jnp.maximum(m_old, jnp.max(s, -1, keepdims=True))
                alpha = jnp.exp2(m_old - m_new)
                p = [
                    jnp.exp2(s[:, i : i + HEAD_WIDTH] - m_new) for i in range(0, KEY_BLOCK, HEAD_WIDTH)
                ]
                m_s[...] = m_new
                l_s[...] = l_s[...] * alpha + functools.reduce(jnp.add, p)
                p = jnp.concatenate(p, 1).astype(jnp.bfloat16)
                acc_s[...] = acc_s[...] * alpha + jnp.dot(p, v, preferred_element_type=jnp.float32)

            return 0

        lax.fori_loop(0, n_key, some_keys, 0)
        if last:
            done = (acc_s[...] / jnp.sum(l_s[...], -1, keepdims=True)).astype(jnp.bfloat16)
            for h in range(n_head):
                heads[at, h * HEAD_WIDTH : (h + 1) * HEAD_WIDTH] = done[h * QUERY_BLOCK : (h + 1) * QUERY_BLOCK]
        else:
            m_out[flat, :] = m_s[...]
            l_out[flat, :] = l_s[...]
            acc_out[flat, :] = acc_s[...]
        return 0

    lax.fori_loop(0, n_query, block, 0)
    if last:
        picked = pick_rows(pick[...], heads[...]).astype(jnp.bfloat16)
        out[...] = picked
        row = 0
        for part in parts:
            part[...] = picked[row : row + part.shape[0], :]
            row += part.shape[0]
    else:
        pick_matrix(order, pick)


def attend(own, q_all, kv_all, keys, order):
    n_head, rows, _ = q_all.shape
    stacked = n_head * QUERY_BLOCK
    n_key = kv_all.shape[0]
    running = jax.ShapeDtypeStruct((n_head * rows, HEAD_WIDTH), jnp.float32)
    return pl.pallas_call(
        functools.partial(attend_kernel, (), False),
        out_shape=(running,) * 3 + (jax.ShapeDtypeStruct((rows, rows), jnp.bfloat16), TOKEN),
        in_specs=[pl.BlockSpec(memory_space=pltpu.SMEM)] + [whole()] * 4,
        out_specs=(whole(),) * 4 + (far_memory(),),
        scratch_shapes=[VMEM((stacked, HEAD_WIDTH), jnp.float32)] * 3
        + [pltpu.SMEM(keys.shape, jnp.int32), pltpu.SemaphoreType.DMA(())],
        compiler_params=params(12),
        cost_estimate=cost(4 * rows * n_key * n_head * HEAD_WIDTH, 4 * rows * n_head * HEAD_WIDTH),
        name="attend",
    )(own, q_all, kv_all, keys, order)


def attend_rest(own, q_all, state, own_keys, pieces, kv_parts, token, pick):
    n_head, rows, _ = q_all.shape
    stacked = n_head * QUERY_BLOCK
    n_key = sum(size for _, size in pieces)
    key_lines = ((n_key + rows) // QUERY_BLOCK, QUERY_BLOCK)
    return pl.pallas_call(
        functools.partial(attend_kernel, tuple(pieces), True),
        out_shape=tuple(
            jax.ShapeDtypeStruct((size, n_head * HEAD_WIDTH), jnp.bfloat16)
            for size in (rows, *part_sizes(rows))
        ),
        in_specs=[pl.BlockSpec(memory_space=pltpu.SMEM)]
        + [whole()] * (5 + len(pieces))
        + [far_memory(), whole()],
        out_specs=(whole(),) * 3,
        scratch_shapes=[
            VMEM((rows, n_head * HEAD_WIDTH), jnp.bfloat16),
            VMEM((n_key, 2 * HEAD_WIDTH), jnp.bfloat16),
            VMEM(key_lines, jnp.int32),
        ]
        + [VMEM((stacked, HEAD_WIDTH), jnp.float32)] * 3
        + [pltpu.SMEM(key_lines, jnp.int32), pltpu.SemaphoreType.DMA(())],
        compiler_params=params(12 + n_key // 512),
        cost_estimate=cost(4 * rows * n_key * n_head * HEAD_WIDTH, 4 * rows * n_head * HEAD_WIDTH),
        name="attend_rest",
    )(own, q_all, *state, own_keys, *kv_parts, token, pick)


def columns_kernel(own, w_out, token_in, near, send_near, far, beside, token, sem):
    del token_in, token
    depth, width = near.shape
    half = depth // 2
    copies = []
    for bits, first, to in (
        (2, own[1] * half, far),
        (3, own[1] * half, beside),
        (1, 0, send_near),
        (0, 0, near),
    ):
        rows = pl.ds(pl.multiple_of(first, half), to.shape[0])
        at = pl.ds(pl.multiple_of(lax.bitwise_xor(own[0], bits) * width, width), width)
        copies.append(pltpu.make_async_copy(w_out.at[rows, at], to, sem.at[len(copies)]))
    start(copies)
    wait(copies)


def columns(own, w_out, token, width):
    rows = w_out.shape[0]
    blocks = [jax.ShapeDtypeStruct((size, width), w_out.dtype) for size in (rows, rows, rows // 2, rows // 2)]
    return pl.pallas_call(
        columns_kernel,
        out_shape=(*blocks, TOKEN),
        in_specs=[pl.BlockSpec(memory_space=pltpu.SMEM), far_memory(), far_memory()],
        out_specs=(whole(),) * 4 + (far_memory(),),
        scratch_shapes=[pltpu.SemaphoreType.DMA((5,))],
        compiler_params=params(6),
        cost_estimate=cost(1, 4 * w_out.size),
        name="columns",
    )(own, w_out, token)


def keep_kernel(pick, own, h0, h1, w0, w1, out, token):
    del token
    total = jnp.dot(h0[...], w0[...], preferred_element_type=jnp.float32)
    total += jnp.dot(h1[...], w1[...], preferred_element_type=jnp.float32)
    out[...] = total + pick_rows(pick[...], own[...])


def keep(pick, own, h0, h1, w0, w1):
    rows, width = own.shape
    depth = h0.shape[1]
    return pl.pallas_call(
        keep_kernel,
        out_shape=(jax.ShapeDtypeStruct((rows, width), jnp.float32), TOKEN),
        in_specs=[whole()] * 6,
        out_specs=(whole(), far_memory()),
        compiler_params=params(12),
        cost_estimate=cost(2 * rows * (2 * depth + rows) * width, 4 * depth * width + 6 * rows * width),
        name="keep",
    )(pick, own, h0, h1, w0, w1)


def shares(own, h):
    half = h.shape[1] // 2
    return tuple(pl.ds(pl.multiple_of(share * half, half), half) for share in (own[1], 1 - own[1]))


def add_heads(total, own, h2, h3, w2, w3, other3):
    mine, others = shares(own, h2)
    for h, columns, weight in ((h2, mine, w2), (h3, mine, w3), (h3, others, other3)):
        total += jnp.dot(h[:, columns], weight[...], preferred_element_type=jnp.float32)
    return total


def gather_kernel(own, token, kept, h2, h3, w2, w3, other3, out):
    del token
    out[...] = add_heads(kept[: h2.shape[0], :], own, h2, h3, w2, w3, other3)


def gather(own, token, kept, h2, h3, w2, w3, other3):
    rows, depth = h2.shape
    width = kept.shape[1]
    return pl.pallas_call(
        gather_kernel,
        out_shape=jax.ShapeDtypeStruct((rows, width), jnp.float32),
        in_specs=[pl.BlockSpec(memory_space=pltpu.SMEM), far_memory()] + [whole()] * 6,
        out_specs=whole(),
        compiler_params=params(14),
        cost_estimate=cost(3 * rows * depth * width, 8 * rows * width),
        name="gather",
    )(own, token, kept, h2, h3, w2, w3, other3)


def finish_kernel(own, most, kept, top2, h2, h3, w2, w3, other3, other2, gain, head, hidden_out, sums):
    first = most.shape[0]
    weight = gain[...].astype(jnp.float32) * head[...].astype(jnp.float32)
    rest = add_heads(kept[first:, :], own, h2, h3, w2, w3, other3)
    for span, h, total in ((slice(0, first), top2, most[...]), (slice(first, kept.shape[0]), h2, rest)):
        _, others = shares(own, h)
        total += jnp.dot(h[:, others], other2[...], preferred_element_type=jnp.float32)
        hidden = total.astype(jnp.bfloat16)
        hidden_out[span, :] = hidden
        x = hidden.astype(jnp.float32)
        for i, terms in enumerate((x * x, x * weight)):
            lanes = functools.reduce(jnp.add, [terms[:, k : k + 128] for k in range(0, terms.shape[1], 128)])
            sums[i : i + 1, span] = jnp.sum(lanes.T, 0, keepdims=True)


def finish(own, most, kept, top2, h2, h3, w2, w3, other3, other2, gain, head):
    rows, width = kept.shape
    depth = h2.shape[1]
    return pl.pallas_call(
        finish_kernel,
        out_shape=(
            jax.ShapeDtypeStruct((rows, width), jnp.bfloat16),
            jax.ShapeDtypeStruct((2, rows), jnp.float32),
        ),
        in_specs=[pl.BlockSpec(memory_space=pltpu.SMEM)] + [whole()] * 11,
        out_specs=(whole(), whole()),
        compiler_params=params(14),
        cost_estimate=cost(2 * rows * depth * width, 8 * rows * width),
        name="finish",
    )(own, most, kept, top2, h2, h3, w2, w3, other3, other2, gain, head)


def flip(x, bit):
    count = lax.axis_size("tensor")
    return lax.ppermute(x, "tensor", [(i, i ^ bit) for i in range(count)])


def swap_parts(x):
    return lax.ppermute(x, "parts", [(0, 1), (1, 0)])


def chunk_sizes(rows, n_dp):
    if n_dp > 8 or rows % 256:
        return (rows,)
    return (rows // 2, rows // 2)


def on_device(
    hidden_in,
    row_loads,
    seg_ids,
    pos_ids,
    prompt_order,
    attn_gain,
    w_query,
    key_matrix,
    value_matrix,
    w_out,
    final_gain,
    value_head,
):
    n_dp = lax.axis_size("dp")
    me = lax.axis_index("dp")
    t = lax.axis_index("tensor")
    rows, width = hidden_in.shape
    sizes = chunk_sizes(rows, n_dp)

    own = [hidden_in[sum(sizes[:c]) : sum(sizes[: c + 1])] for c in range(len(sizes))]
    across = [flip(x, 2) for x in own]
    pair = flip(hidden_in, 1)

    lines = rows // QUERY_BLOCK
    digits, cos, sin = prep(
        row_loads, seg_ids.reshape(lines, QUERY_BLOCK), pos_ids.reshape(lines, QUERY_BLOCK)
    )
    gain = attn_gain.reshape(1, -1)
    t_own = jnp.stack([t, lax.axis_index("parts"), me]).astype(jnp.int32)
    acc, squares, far_weights, token = early(
        t_own, hidden_in, pair, gain, w_query, key_matrix, value_matrix
    )

    near, send_near, far2, far3, token = columns(t_own, w_out, token, width)
    near_other = flip(send_near, 1)

    q_parts, kv_parts = [], [[] for _ in range(n_dp)]
    for c in range(len(sizes)):
        received, token = lax.optimization_barrier((across[c], token))
        if c == len(sizes) - 1:
            far2, far3, token = lax.optimization_barrier((far2, far3, token))
            far2, far3 = flip(far2, 2), flip(far3, 3)
        if c > 0:
            for d in range(1, n_dp):
                kv_parts[d][-1], token = lax.optimization_barrier((kv_parts[d][-1], token))
        received, token = lax.optimization_barrier((received, token))
        diagonal = flip(received, 1)
        if c > 0:
            near_other, token = lax.optimization_barrier((near_other, token))
        last = c == len(sizes) - 1
        soon = [(0, i) for i in range(c)] + [(d, i) for d in range(1, n_dp) for i in range(c)] if last else []
        q, kv, *side, token = late(
            sum(sizes[:c]),
            t_own,
            token,
            acc,
            squares,
            received,
            diagonal,
            gain,
            far_weights,
            cos,
            sin,
            digits,
            last,
            q_parts if last else [],
            [(d, sizes[i]) for d, i in soon],
            [kv_parts[d][i] for d, i in soon],
        )
        q_parts.append(q)
        kv_parts[0].append(kv)
        for d in range(1, n_dp):
            kv_parts[d].append(lax.ppermute(kv, "dp", [(i, (i + d) % n_dp) for i in range(n_dp)]))

    order = prompt_order.reshape(1, rows)
    q_all, (kv_all, keys) = q, side
    *state, pick, token = attend(t_own, q_all, kv_all, keys, order)
    far3, token = lax.optimization_barrier((far3, token))
    other3 = swap_parts(far3)
    heads, *parts = attend_rest(
        t_own,
        q_all,
        state,
        keys,
        [(d, sizes[-1]) for d in range(1, n_dp)],
        [kv_parts[d][-1] for d in range(1, n_dp)],
        token,
        pick,
    )
    heads2 = [flip(parts[0], 2)]
    rest, far2 = lax.optimization_barrier((parts[1], far2))
    heads2.append(flip(rest, 2))
    other2 = swap_parts(far2)
    heads_other = flip(heads, 1)
    heads_other, other3 = lax.optimization_barrier((heads_other, other3))
    kept, token = keep(pick, hidden_in, heads, heads_other, near, near_other)
    heads2[0], token = lax.optimization_barrier((heads2[0], token))
    heads3 = [flip(x, 1) for x in heads2]
    most = gather(t_own, token, kept, heads2[0], heads3[0], far2, far3, other3)
    hidden, sums = finish(
        t_own,
        most,
        kept,
        heads2[0],
        heads2[1],
        heads3[1],
        far2,
        far3,
        other3,
        other2,
        final_gain.reshape(1, width),
        value_head.reshape(1, width),
    )
    square, product = sums + flip(sums, 1) + (flip(sums, 2) + flip(sums, 3))
    return hidden, product * lax.rsqrt(square / MODEL_WIDTH + NORM_EPS)


def solution(mesh):
    return jax.shard_map(
        on_device,
        mesh=mesh,
        in_specs=(
            P(("parts", "dp"), "tensor"),
            P(("parts", "dp"), None),
            P(("parts", "dp")),
            P(("parts", "dp")),
            P(("parts", "dp"), None),
            P(),
            P(None, "tensor"),
            P(None, "tensor"),
            P(None, "tensor"),
            P("tensor", None),
            P("tensor"),
            P("tensor"),
        ),
        out_specs=(P(("parts", "dp"), "tensor"), P(("parts", "dp"))),
        check_vma=False,
    )
```

```python
import functools
import math

import jax
import jax.numpy as jnp
from jax import lax
from jax.experimental import pallas as pl
from jax.experimental.pallas import tpu as pltpu
from jax.sharding import PartitionSpec as P

MODEL_WIDTH = 4096
HEAD_WIDTH = 128
NORM_EPS = 1e-05
ROPE_BASE = 500000.0

SEG_SPAN = 64
POS_SPAN = 1024
POS_DIGIT = 128
DIGIT_ROWS = 16

QUERY_BLOCK = 128
KEY_BLOCK = 256
MASKED = -1e30

VMEM = pltpu.VMEM
EARLY_MIB = 16
TOKEN = jax.ShapeDtypeStruct((8, 128), jnp.float32)


def params(limit_mib):
    return pltpu.CompilerParams(vmem_limit_bytes=limit_mib * 2**20)


def cost(flops, bytes_accessed):
    return pl.CostEstimate(flops=flops, bytes_accessed=bytes_accessed, transcendentals=0)


def whole():
    return pl.BlockSpec(memory_space=VMEM)


def far_memory():
    return pl.BlockSpec(memory_space=pltpu.HBM)


def prep_kernel(loads, seg, pos, digits, cos, sin):
    lines, lanes = seg.shape
    row = lanes * lax.broadcasted_iota(jnp.int32, seg.shape, 0) + lax.broadcasted_iota(jnp.int32, seg.shape, 1)
    dest = jnp.zeros(seg.shape, jnp.int32)
    total = 0
    for e in range(loads.shape[1]):
        total = total + loads[0, e]
        dest += jnp.where(row >= total, 1, 0)
    low_pos = lax.bitwise_and(pos[...], POS_DIGIT - 1)
    high_pos = lax.shift_right_logical(pos[...], POS_DIGIT.bit_length() - 1)
    digits[...] = jnp.zeros(digits.shape, digits.dtype)
    for j, digit in enumerate((low_pos, high_pos, seg[...], dest)):
        line = jnp.concatenate([digit[i : i + 1, :] for i in range(lines)], 1)
        digits[j : j + 1, :] = line.astype(jnp.float32).astype(digits.dtype)
    at = pos[...].astype(jnp.float32)
    half = HEAD_WIDTH // 2
    lane = lax.broadcasted_iota(jnp.int32, (lanes, HEAD_WIDTH), 1)
    low = lane < half
    power = jnp.where(low, lane, lane - half).astype(jnp.float32)
    inverse = jnp.exp(power * (-2.0 * math.log(ROPE_BASE) / HEAD_WIDTH))
    for i in range(lines):
        column = jnp.broadcast_to(at[i : i + 1, :], (lanes, lanes)).T
        angle = column * inverse
        span = slice(i * lanes, (i + 1) * lanes)
        sine = jnp.sin(angle)
        cos[span, :] = jnp.cos(angle)
        sin[span, :] = jnp.where(low, -sine, sine)


def prep(row_loads, seg, pos):
    lines, lanes = seg.shape
    rows = lines * lanes
    table = jax.ShapeDtypeStruct((rows, HEAD_WIDTH), jnp.float32)
    return pl.pallas_call(
        prep_kernel,
        out_shape=(jax.ShapeDtypeStruct((DIGIT_ROWS, rows), jnp.bfloat16), table, table),
        in_specs=[pl.BlockSpec(memory_space=pltpu.SMEM), whole(), whole()],
        out_specs=(whole(), whole(), whole()),
        compiler_params=params(6),
        cost_estimate=cost(2 * 10**9, 4 * 10**7),
        name="prep",
    )(row_loads, seg, pos)


def gained(piece, gain, number):
    x = piece[...].astype(jnp.float32)
    width = x.shape[1]
    factor = gain[:, pl.ds(pl.multiple_of(number * width, width), width)].astype(jnp.float32)
    return jnp.sum(x * x, -1, keepdims=True), (x * factor).astype(jnp.bfloat16)


def weight_copies(weights, to, sem, ids, width):
    copies = []
    for i, number in enumerate(ids):
        at = 0
        rows = pl.ds(pl.multiple_of(number * width, width), width)
        for weight in weights:
            columns = pl.ds(at, weight.shape[1])
            copies.append(pltpu.make_async_copy(weight.at[rows, :], to.at[i, :, columns], sem.at[len(copies)]))
            at += weight.shape[1]
    return copies


def start(copies):
    for copy in copies:
        copy.start()


def wait(copies):
    for copy in copies:
        copy.wait()


def early_kernel(own, r0, r1, gain, wq, wk, wv, acc, squares, far_weights, token, held, sem):
    del token
    width = r0.shape[1]
    t = own[0]
    near = weight_copies((wq, wk, wv), held, sem.at[0], (t, lax.bitwise_xor(t, 1)), width)
    far = weight_copies(
        (wq, wk, wv), far_weights, sem.at[1], (lax.bitwise_xor(t, 2), lax.bitwise_xor(t, 3)), width
    )
    start(near)
    start(far)
    square0, x0 = gained(r0, gain, t)
    wait(near[:3])
    acc[...] = jnp.dot(x0, held[0], preferred_element_type=jnp.float32)
    square1, x1 = gained(r1, gain, lax.bitwise_xor(t, 1))
    wait(near[3:])
    acc[...] += jnp.dot(x1, held[1], preferred_element_type=jnp.float32)
    squares[...] = square0 + square1
    wait(far)


def early(own, r0, r1, gain, wq, wk, wv):
    rows, width = r0.shape
    columns = wq.shape[1] + wk.shape[1] + wv.shape[1]
    half = (2, width, columns)
    return pl.pallas_call(
        early_kernel,
        out_shape=(
            jax.ShapeDtypeStruct((rows, columns), jnp.float32),
            jax.ShapeDtypeStruct((rows, 1), jnp.float32),
            jax.ShapeDtypeStruct(half, jnp.bfloat16),
            TOKEN,
        ),
        in_specs=[pl.BlockSpec(memory_space=pltpu.SMEM)] + [whole()] * 3 + [far_memory()] * 3,
        out_specs=(whole(), whole(), whole(), far_memory()),
        scratch_shapes=[VMEM(half, jnp.bfloat16), pltpu.SemaphoreType.DMA((2, 6))],
        compiler_params=params(12),
        cost_estimate=cost(4 * rows * width * columns, 8 * width * columns),
        name="early",
    )(own, r0, r1, gain, wq, wk, wv)


def digit_lines(rows):
    return [(i, min(2 * HEAD_WIDTH, rows - i)) for i in range(0, rows, 2 * HEAD_WIDTH)]


def keys_of(digits, back, own):
    digit = digits.astype(jnp.float32).astype(jnp.int32)
    doc = digit[3:4] * SEG_SPAN + digit[2:3]
    key = doc * POS_SPAN + digit[1:2] * POS_DIGIT + digit[0:1]
    return jnp.where(back <= own[2], key, -1)


def unpack(pieces, sources, own, kv_all, keys):
    lanes = keys.shape[1]
    row = 0
    for (back, size), source in zip(pieces, sources, strict=True):
        kv_all[row : row + size, :] = source[:size, :]
        for i, (line, count) in enumerate(digit_lines(size)):
            at = size + i * DIGIT_ROWS
            key = keys_of(source[at : at + DIGIT_ROWS, :count], back, own)
            for j in range(0, count, lanes):
                to = (row + line + j) // lanes
                keys[to : to + 1, :] = key[:, j : j + lanes]
        row += size


def late_kernel(at, pieces, own, before, acc, squares, r2, r3, gain, weights, cos, sin, digits, *refs):
    del before
    refs = list(refs)
    rows = r2.shape[0]
    n_old = sum(1 for back, _ in pieces if back == 0)
    q_old, kv_old = refs[:n_old], refs[n_old : n_old + len(pieces)]
    q_out, kv_out, *outs = refs[n_old + len(pieces) :]
    span = slice(at, at + rows)
    square2, x2 = gained(r2, gain, lax.bitwise_xor(own[0], 2))
    total = acc[span, :] + jnp.dot(x2, weights[0], preferred_element_type=jnp.float32)
    square3, x3 = gained(r3, gain, lax.bitwise_xor(own[0], 3))
    total += jnp.dot(x3, weights[1], preferred_element_type=jnp.float32)
    total *= lax.rsqrt((squares[span, :] + square2 + square3) / MODEL_WIDTH + NORM_EPS)
    cosine, sine = cos[span, :], sin[span, :]
    n_head = q_out.shape[0]

    def rope(x):
        return (x * cosine + pltpu.roll(x, HEAD_WIDTH // 2, 1) * sine).astype(jnp.bfloat16)

    here = slice(at, at + rows) if q_out.shape[1] > rows else slice(0, rows)
    for h in range(n_head):
        q_out[h, here, :] = rope(total[:, h * HEAD_WIDTH : (h + 1) * HEAD_WIDTH])
    kv_out[:rows, :HEAD_WIDTH] = rope(total[:, n_head * HEAD_WIDTH : (n_head + 1) * HEAD_WIDTH])
    kv_out[:rows, HEAD_WIDTH:] = total[:, (n_head + 1) * HEAD_WIDTH :].astype(jnp.bfloat16)
    for i, (line, count) in enumerate(digit_lines(rows)):
        to = rows + i * DIGIT_ROWS
        kv_out[to : to + DIGIT_ROWS, :count] = digits[:, at + line : at + line + count]
    if len(outs) > 1:
        kv_all, keys, _ = outs
        row = 0
        for q in q_old:
            q_out[:, row : row + q.shape[1], :] = q[...]
            row += q.shape[1]
        sources = [*kv_old[:n_old], kv_out, *kv_old[n_old:]]
        unpack([*pieces[:n_old], (0, rows), *pieces[n_old:]], sources, own, kv_all, keys)


def late(at, own, before, acc, squares, r2, r3, gain, weights, cos, sin, digits, last, q_old, pieces, kv_old):
    rows, width = r2.shape
    columns = acc.shape[1]
    heads = columns // HEAD_WIDTH - 2
    n_key = rows + sum(size for _, size in pieces)
    more, specs = (), ()
    if last:
        more = (
            jax.ShapeDtypeStruct((n_key, 2 * HEAD_WIDTH), jnp.bfloat16),
            jax.ShapeDtypeStruct((n_key // QUERY_BLOCK, QUERY_BLOCK), jnp.int32),
        )
        specs = (whole(), whole())
    return pl.pallas_call(
        functools.partial(late_kernel, at, tuple(pieces)),
        out_shape=(
            jax.ShapeDtypeStruct((heads, at + rows if last else rows, HEAD_WIDTH), jnp.bfloat16),
            jax.ShapeDtypeStruct((rows + DIGIT_ROWS * len(digit_lines(rows)), 2 * HEAD_WIDTH), jnp.bfloat16),
            *more,
            TOKEN,
        ),
        in_specs=[pl.BlockSpec(memory_space=pltpu.SMEM), far_memory()]
        + [whole()] * (9 + len(q_old) + len(kv_old)),
        out_specs=(whole(), whole(), *specs, far_memory()),
        compiler_params=params(10),
        cost_estimate=cost(4 * rows * width * columns, 4 * width * columns),
        name="late",
    )(own, before, acc, squares, r2, r3, gain, weights, cos, sin, digits, *q_old, *kv_old)


def part_sizes(rows):
    return (rows // 2, rows // 2)


def pick_matrix(order, out):
    rows = out.shape[0]
    size = QUERY_BLOCK
    for i in range(0, rows, size):
        wanted = jnp.broadcast_to(order[:, i : i + size], (size, size)).T
        for j in range(0, rows, size):
            at = lax.broadcasted_iota(jnp.int32, (size, size), 1) + j
            out[i : i + size, j : j + size] = jnp.where(wanted == at, 1.0, 0.0).astype(out.dtype)


def pick_rows(pick, x):
    return jnp.dot(pick, x, preferred_element_type=jnp.float32)


def attend_kernel(pieces, last, own, q_all, *refs):
    refs = list(refs)

    def take(count):
        taken = refs[:count]
        del refs[:count]
        return taken

    n_head, rows, _ = q_all.shape
    n_query = rows // QUERY_BLOCK
    if last:
        m_in, l_in, acc_in, own_keys = take(4)
        kv_in = take(len(pieces))
        _, pick, out, *parts = take(5)
        heads, kv_all, keys = take(3)
        unpack(pieces, kv_in, own, kv_all, keys)
        own_line = kv_all.shape[0] // QUERY_BLOCK
        keys[own_line : own_line + n_query, :] = own_keys[:n_query, :]
    else:
        kv_all, keys, order, m_out, l_out, acc_out, pick, _ = take(8)
        own_line = 0
    m_s, l_s, acc_s, keys_s, sem = refs
    n_key = kv_all.shape[0] // KEY_BLOCK
    lanes = keys.shape[1]
    copy = pltpu.make_async_copy(keys, keys_s, sem)
    copy.start()
    copy.wait()
    scale = 1.4426950408889634 / HEAD_WIDTH**0.5
    stacked = n_head * QUERY_BLOCK
    lines = KEY_BLOCK // lanes

    def block(qb, _):
        at = pl.ds(pl.multiple_of(qb * QUERY_BLOCK, QUERY_BLOCK), QUERY_BLOCK)
        flat = pl.ds(pl.multiple_of(qb * stacked, stacked), stacked)
        q = q_all[:, at, :].reshape(stacked, HEAD_WIDTH)
        high = jnp.broadcast_to(keys[pl.ds(own_line + qb, 1), :], (QUERY_BLOCK, lanes)).T
        low = high - lax.bitwise_and(high, POS_SPAN - 1)
        high, low = (jnp.concatenate([x] * lines, 1) for x in (high, low))
        lowest = keys_s[own_line + qb, 0]
        lowest = lowest - lax.bitwise_and(lowest, POS_SPAN - 1)
        highest = lax.bitwise_or(keys_s[own_line + qb, lanes - 1], POS_SPAN - 1)
        if not last:
            m_s[...] = jnp.full(m_s.shape, MASKED, jnp.float32)
            l_s[...] = jnp.zeros(l_s.shape, jnp.float32)
            acc_s[...] = jnp.zeros(acc_s.shape, jnp.float32)
        else:
            m_s[...] = m_in[flat, :]
            l_s[...] = l_in[flat, :]
            acc_s[...] = acc_in[flat, :]

        def some_keys(index, _):
            @pl.when((keys_s[index * lines + lines - 1, lanes - 1] >= lowest) & (keys_s[index * lines, 0] <= highest))
            def _():
                span = pl.ds(pl.multiple_of(index * KEY_BLOCK, KEY_BLOCK), KEY_BLOCK)
                k = kv_all[span, :HEAD_WIDTH]
                v = kv_all[span, HEAD_WIDTH:]
                s = lax.dot_general(q, k, (((1,), (1,)), ((), ())), preferred_element_type=jnp.float32)
                ids = jnp.concatenate([keys[pl.ds(index * lines + i, 1), :] for i in range(lines)], 1)
                allowed = (ids <= high) & (ids >= low)
                s = jnp.where(allowed[None], (s * scale).reshape(n_head, QUERY_BLOCK, KEY_BLOCK), MASKED)
                s = s.reshape(stacked, KEY_BLOCK)
                m_old = m_s[...]
                m_new = jnp.maximum(m_old, jnp.max(s, -1, keepdims=True))
                alpha = jnp.exp2(m_old - m_new)
                p = [
                    jnp.exp2(s[:, i : i + HEAD_WIDTH] - m_new) for i in range(0, KEY_BLOCK, HEAD_WIDTH)
                ]
                m_s[...] = m_new
                l_s[...] = l_s[...] * alpha + functools.reduce(jnp.add, p)
                p = jnp.concatenate(p, 1).astype(jnp.bfloat16)
                acc_s[...] = acc_s[...] * alpha + jnp.dot(p, v, preferred_element_type=jnp.float32)

            return 0

        lax.fori_loop(0, n_key, some_keys, 0)
        if last:
            done = (acc_s[...] / jnp.sum(l_s[...], -1, keepdims=True)).astype(jnp.bfloat16)
            for h in range(n_head):
                heads[at, h * HEAD_WIDTH : (h + 1) * HEAD_WIDTH] = done[h * QUERY_BLOCK : (h + 1) * QUERY_BLOCK]
        else:
            m_out[flat, :] = m_s[...]
            l_out[flat, :] = l_s[...]
            acc_out[flat, :] = acc_s[...]
        return 0

    lax.fori_loop(0, n_query, block, 0)
    if last:
        picked = pick_rows(pick[...], heads[...]).astype(jnp.bfloat16)
        out[...] = picked
        row = 0
        for part in parts:
            part[...] = picked[row : row + part.shape[0], :]
            row += part.shape[0]
    else:
        pick_matrix(order, pick)


def attend(own, q_all, kv_all, keys, order):
    n_head, rows, _ = q_all.shape
    stacked = n_head * QUERY_BLOCK
    n_key = kv_all.shape[0]
    running = jax.ShapeDtypeStruct((n_head * rows, HEAD_WIDTH), jnp.float32)
    return pl.pallas_call(
        functools.partial(attend_kernel, (), False),
        out_shape=(running,) * 3 + (jax.ShapeDtypeStruct((rows, rows), jnp.bfloat16), TOKEN),
        in_specs=[pl.BlockSpec(memory_space=pltpu.SMEM)] + [whole()] * 4,
        out_specs=(whole(),) * 4 + (far_memory(),),
        scratch_shapes=[VMEM((stacked, HEAD_WIDTH), jnp.float32)] * 3
        + [pltpu.SMEM(keys.shape, jnp.int32), pltpu.SemaphoreType.DMA(())],
        compiler_params=params(12),
        cost_estimate=cost(4 * rows * n_key * n_head * HEAD_WIDTH, 4 * rows * n_head * HEAD_WIDTH),
        name="attend",
    )(own, q_all, kv_all, keys, order)


def attend_rest(own, q_all, state, own_keys, pieces, kv_parts, token, pick):
    n_head, rows, _ = q_all.shape
    stacked = n_head * QUERY_BLOCK
    n_key = sum(size for _, size in pieces)
    key_lines = ((n_key + rows) // QUERY_BLOCK, QUERY_BLOCK)
    return pl.pallas_call(
        functools.partial(attend_kernel, tuple(pieces), True),
        out_shape=tuple(
            jax.ShapeDtypeStruct((size, n_head * HEAD_WIDTH), jnp.bfloat16)
            for size in (rows, *part_sizes(rows))
        ),
        in_specs=[pl.BlockSpec(memory_space=pltpu.SMEM)]
        + [whole()] * (5 + len(pieces))
        + [far_memory(), whole()],
        out_specs=(whole(),) * 3,
        scratch_shapes=[
            VMEM((rows, n_head * HEAD_WIDTH), jnp.bfloat16),
            VMEM((n_key, 2 * HEAD_WIDTH), jnp.bfloat16),
            VMEM(key_lines, jnp.int32),
        ]
        + [VMEM((stacked, HEAD_WIDTH), jnp.float32)] * 3
        + [pltpu.SMEM(key_lines, jnp.int32), pltpu.SemaphoreType.DMA(())],
        compiler_params=params(12 + n_key // 512),
        cost_estimate=cost(4 * rows * n_key * n_head * HEAD_WIDTH, 4 * rows * n_head * HEAD_WIDTH),
        name="attend_rest",
    )(own, q_all, *state, own_keys, *kv_parts, token, pick)


def columns_kernel(own, w_out, token_in, near, send_near, far, beside, token, sem):
    del token_in, token
    depth, width = near.shape
    half = depth // 2
    copies = []
    for bits, first, to in (
        (2, own[1] * half, far),
        (3, own[1] * half, beside),
        (1, 0, send_near),
        (0, 0, near),
    ):
        rows = pl.ds(pl.multiple_of(first, half), to.shape[0])
        at = pl.ds(pl.multiple_of(lax.bitwise_xor(own[0], bits) * width, width), width)
        copies.append(pltpu.make_async_copy(w_out.at[rows, at], to, sem.at[len(copies)]))
    start(copies)
    wait(copies)


def columns(own, w_out, token, width):
    rows = w_out.shape[0]
    blocks = [jax.ShapeDtypeStruct((size, width), w_out.dtype) for size in (rows, rows, rows // 2, rows // 2)]
    return pl.pallas_call(
        columns_kernel,
        out_shape=(*blocks, TOKEN),
        in_specs=[pl.BlockSpec(memory_space=pltpu.SMEM), far_memory(), far_memory()],
        out_specs=(whole(),) * 4 + (far_memory(),),
        scratch_shapes=[pltpu.SemaphoreType.DMA((5,))],
        compiler_params=params(6),
        cost_estimate=cost(1, 4 * w_out.size),
        name="columns",
    )(own, w_out, token)


def keep_kernel(pick, own, h0, h1, w0, w1, top, bottom, token):
    del token
    total = jnp.dot(h0[...], w0[...], preferred_element_type=jnp.float32)
    total += jnp.dot(h1[...], w1[...], preferred_element_type=jnp.float32)
    total += pick_rows(pick[...], own[...])
    top[...] = total[: top.shape[0], :]
    bottom[...] = total[top.shape[0] :, :]


def keep(pick, own, h0, h1, w0, w1):
    rows, width = own.shape
    depth = h0.shape[1]
    return pl.pallas_call(
        keep_kernel,
        out_shape=(*(jax.ShapeDtypeStruct((size, width), jnp.float32) for size in part_sizes(rows)), TOKEN),
        in_specs=[whole()] * 6,
        out_specs=(whole(), whole(), far_memory()),
        compiler_params=params(12),
        cost_estimate=cost(2 * rows * (2 * depth + rows) * width, 4 * depth * width + 6 * rows * width),
        name="keep",
    )(pick, own, h0, h1, w0, w1)


def shares(own, h):
    half = h.shape[1] // 2
    return tuple(pl.ds(pl.multiple_of(share * half, half), half) for share in (own[1], 1 - own[1]))


def add_heads(total, own, h2, h3, w2, w3, other3):
    mine, others = shares(own, h2)
    for h, columns, weight in ((h2, mine, w2), (h3, mine, w3), (h3, others, other3)):
        total += jnp.dot(h[:, columns], weight[...], preferred_element_type=jnp.float32)
    return total


def gather_kernel(own, token_in, kept, h2, h3, w2, w3, other3, out, token):
    del token_in, token
    out[...] = add_heads(kept[...], own, h2, h3, w2, w3, other3)


def gather(own, token, kept, h2, h3, w2, w3, other3):
    rows, depth = h2.shape
    width = kept.shape[1]
    return pl.pallas_call(
        gather_kernel,
        out_shape=(jax.ShapeDtypeStruct((rows, width), jnp.float32), TOKEN),
        in_specs=[pl.BlockSpec(memory_space=pltpu.SMEM), far_memory()] + [whole()] * 6,
        out_specs=(whole(), far_memory()),
        compiler_params=params(14),
        cost_estimate=cost(3 * rows * depth * width, 8 * rows * width),
        name="gather",
    )(own, token, kept, h2, h3, w2, w3, other3)


def finish_kernel(own, most0, most1, top2, h2, other2, gain, head, hidden_out, sums):
    weight = gain[...].astype(jnp.float32) * head[...].astype(jnp.float32)
    first = most0.shape[0]
    for span, h, most in ((slice(0, first), top2, most0), (slice(first, first + most1.shape[0]), h2, most1)):
        _, others = shares(own, h)
        total = most[...] + jnp.dot(h[:, others], other2[...], preferred_element_type=jnp.float32)
        hidden = total.astype(jnp.bfloat16)
        hidden_out[span, :] = hidden
        x = hidden.astype(jnp.float32)
        for i, terms in enumerate((x * x, x * weight)):
            lanes = functools.reduce(jnp.add, [terms[:, k : k + 128] for k in range(0, terms.shape[1], 128)])
            sums[i : i + 1, span] = jnp.sum(lanes.T, 0, keepdims=True)


def finish(own, most0, most1, top2, h2, other2, gain, head):
    rows, width = most0.shape[0] + most1.shape[0], most0.shape[1]
    depth = h2.shape[1]
    return pl.pallas_call(
        finish_kernel,
        out_shape=(
            jax.ShapeDtypeStruct((rows, width), jnp.bfloat16),
            jax.ShapeDtypeStruct((2, rows), jnp.float32),
        ),
        in_specs=[pl.BlockSpec(memory_space=pltpu.SMEM)] + [whole()] * 7,
        out_specs=(whole(), whole()),
        compiler_params=params(14),
        cost_estimate=cost(rows * depth * width, 8 * rows * width),
        name="finish",
    )(own, most0, most1, top2, h2, other2, gain, head)


def flip(x, bit):
    count = lax.axis_size("tensor")
    return lax.ppermute(x, "tensor", [(i, i ^ bit) for i in range(count)])


def swap_parts(x):
    return lax.ppermute(x, "parts", [(0, 1), (1, 0)])


def chunk_sizes(rows, n_dp):
    if n_dp > 8 or rows % 256:
        return (rows,)
    return (rows // 2, rows // 2)


def on_device(
    hidden_in,
    row_loads,
    seg_ids,
    pos_ids,
    prompt_order,
    attn_gain,
    w_query,
    key_matrix,
    value_matrix,
    w_out,
    final_gain,
    value_head,
):
    n_dp = lax.axis_size("dp")
    me = lax.axis_index("dp")
    t = lax.axis_index("tensor")
    rows, width = hidden_in.shape
    sizes = chunk_sizes(rows, n_dp)

    own = [hidden_in[sum(sizes[:c]) : sum(sizes[: c + 1])] for c in range(len(sizes))]
    across = [flip(x, 2) for x in own]
    pair = flip(hidden_in, 1)

    lines = rows // QUERY_BLOCK
    digits, cos, sin = prep(
        row_loads, seg_ids.reshape(lines, QUERY_BLOCK), pos_ids.reshape(lines, QUERY_BLOCK)
    )
    gain = attn_gain.reshape(1, -1)
    t_own = jnp.stack([t, lax.axis_index("parts"), me]).astype(jnp.int32)
    acc, squares, far_weights, token = early(
        t_own, hidden_in, pair, gain, w_query, key_matrix, value_matrix
    )

    near, send_near, far2, far3, token = columns(t_own, w_out, token, width)
    near_other = flip(send_near, 1)

    q_parts, kv_parts = [], [[] for _ in range(n_dp)]
    for c in range(len(sizes)):
        received, token = lax.optimization_barrier((across[c], token))
        if c == len(sizes) - 1:
            far2, far3, token = lax.optimization_barrier((far2, far3, token))
            far2, far3 = flip(far2, 2), flip(far3, 3)
        if c > 0:
            for d in range(1, n_dp):
                kv_parts[d][-1], token = lax.optimization_barrier((kv_parts[d][-1], token))
        received, token = lax.optimization_barrier((received, token))
        diagonal = flip(received, 1)
        if c > 0:
            near_other, token = lax.optimization_barrier((near_other, token))
        last = c == len(sizes) - 1
        soon = [(0, i) for i in range(c)] + [(d, i) for d in range(1, n_dp) for i in range(c)] if last else []
        q, kv, *side, token = late(
            sum(sizes[:c]),
            t_own,
            token,
            acc,
            squares,
            received,
            diagonal,
            gain,
            far_weights,
            cos,
            sin,
            digits,
            last,
            q_parts if last else [],
            [(d, sizes[i]) for d, i in soon],
            [kv_parts[d][i] for d, i in soon],
        )
        q_parts.append(q)
        kv_parts[0].append(kv)
        for d in range(1, n_dp):
            kv_parts[d].append(lax.ppermute(kv, "dp", [(i, (i + d) % n_dp) for i in range(n_dp)]))

    order = prompt_order.reshape(1, rows)
    q_all, (kv_all, keys) = q, side
    *state, pick, token = attend(t_own, q_all, kv_all, keys, order)
    far3, token = lax.optimization_barrier((far3, token))
    other3 = swap_parts(far3)
    heads, *parts = attend_rest(
        t_own,
        q_all,
        state,
        keys,
        [(d, sizes[-1]) for d in range(1, n_dp)],
        [kv_parts[d][-1] for d in range(1, n_dp)],
        token,
        pick,
    )
    heads2 = [flip(parts[0], 2)]
    rest, far2 = lax.optimization_barrier((parts[1], far2))
    heads2.append(flip(rest, 2))
    other2 = swap_parts(far2)
    heads_other = flip(heads, 1)
    heads_other, other3 = lax.optimization_barrier((heads_other, other3))
    kept0, kept1, token = keep(pick, hidden_in, heads, heads_other, near, near_other)
    heads2[0], token = lax.optimization_barrier((heads2[0], token))
    heads3 = [flip(x, 1) for x in heads2]
    most0, token = gather(t_own, token, kept0, heads2[0], heads3[0], far2, far3, other3)
    most1, _ = gather(t_own, token, kept1, heads2[1], heads3[1], far2, far3, other3)
    hidden, sums = finish(
        t_own, most0, most1, *heads2, other2, final_gain.reshape(1, width), value_head.reshape(1, width)
    )
    square, product = sums + flip(sums, 1) + (flip(sums, 2) + flip(sums, 3))
    return hidden, product * lax.rsqrt(square / MODEL_WIDTH + NORM_EPS)


def solution(mesh):
    return jax.shard_map(
        on_device,
        mesh=mesh,
        in_specs=(
            P(("parts", "dp"), "tensor"),
            P(("parts", "dp"), None),
            P(("parts", "dp")),
            P(("parts", "dp")),
            P(("parts", "dp"), None),
            P(),
            P(None, "tensor"),
            P(None, "tensor"),
            P(None, "tensor"),
            P("tensor", None),
            P("tensor"),
            P("tensor"),
        ),
        out_specs=(P(("parts", "dp"), "tensor"), P(("parts", "dp"))),
        check_vma=False,
    )
```
